128 devices in a mesh: ctx: 32 (over x, z, core), head: 4 (over y).
Axes of the slice: x: 4, y: 4, z: 4, core: 2. Of those that a mesh axis runs over, the one named last changes fastest.
Arguments:
- queries: bfloat16 [16384, 2048], P(('ctx', 'head')), may hold values from -240 to 240
- keys_in: bfloat16 [16384, 2048], P(('ctx', 'head')), may hold values from -8 to 8
- values: bfloat16 [16384, 2048], P(('ctx', 'head')), may hold values from -6 to 6
- out_grad: bfloat16 [16384, 2048], P(('ctx', 'head')), may hold values from -6 to 6
- doc_lengths: int32 [15], replicated, may hold values from 1 to 2048, 16384 in all
Outputs:
- attended: bfloat16 [16384, 2048], P(('ctx', 'head'))
- query_grad: bfloat16 [16384, 2048], P(('ctx', 'head'))
- key_grad: bfloat16 [16384, 2048], P(('ctx', 'head'))
- value_grad: bfloat16 [16384, 2048], P(('ctx', 'head'))
The draws below stay inside these ranges and needn't reach their ends.
Inputs may be any that keep to these rules, and one draw needn't show every extreme that they name: `doc_lengths`: each document has 1 to 2048 tokens, the longest exactly 2048; the lengths sum to 16384.
All inputs are finite; a program needn't handle non-finite values.
Results may differ from the reference program's by a relative error of at most 0.035.
Values may be sent and summed in bfloat16 or wider, within the bound.
A program may use at most 192 MiB of HBM per device.

```python
import math
import jax
import jax.numpy as jnp
import numpy as np
from jax import lax

HEADS = 16
HEAD_DIM = 128
TOK_DEV = 512
REACH = 4
TOKENS = 16384
MAXDOC = 2048
NDOCS = 15


def shared_keys(key):
    base = jax.random.normal(jax.random.fold_in(key, 11), (TOKENS, HEADS * HEAD_DIM), jnp.float32)
    return jnp.clip(base, -6.0, 6.0)


def draw_keys_in(key, part):
    base = shared_keys(key)
    key = jax.random.fold_in(key, 2)
    fresh = jnp.clip(jax.random.normal(key, base.shape, jnp.float32), -6.0, 6.0)
    return (base + 0.3 * fresh).astype(jnp.bfloat16)


def draw_queries(key, part):
    base = shared_keys(key)
    key = jax.random.fold_in(key, 1)
    noise = jnp.clip(jax.random.normal(key, base.shape, jnp.float32), -6.0, 6.0)
    return noise.astype(jnp.bfloat16)


def levels(rng, shape, shards, least, high):
    factor_of = 1.0
    for dim, parts in shards:
        draws = jax.random.uniform(jax.random.fold_in(jax.random.fold_in(rng, 6), dim), (parts,), jnp.float32, least / len(shards), high / len(shards))
        factor_of = factor_of * jnp.repeat(jnp.exp(draws), shape[dim] // parts).reshape((-1,) + (1,) * (len(shape) - 1 - dim))
    return factor_of


def length_profile(number_of, total, most, skew):
    portions = [(1 << 20) // math.isqrt(grade ** skew) + 1 for grade in range(2, number_of + 1)]
    surplus, counts = total - most - (number_of - 1), [1] * (number_of - 1)
    while surplus > 0:
        free = [i for i in range(number_of - 1) if counts[i] < most]
        whole, budget = sum([portions[i] for i in free]), surplus
        for i in free:
            more = min(most - counts[i], max(1, budget * portions[i] // whole), surplus)
            counts[i] = counts[i] + more
            surplus = surplus - more
    return np.array([most] + counts)


def uneven(stream_key, count, total, most, slope):
    if count == 2:
        one = jax.random.randint(stream_key, (), max(1, total - most), min(most, total - 1) + 1)
        return jnp.stack([one, total - one])
    lengths = jnp.asarray(length_profile(count, total, most, slope), jnp.int32)
    couples = (count - 1) // 2
    giver, taker = lengths[1:1 + 2 * couples:2], lengths[2:2 + 2 * couples:2]
    room = jnp.minimum(giver - 1, most - taker)
    shifted = jax.random.randint(jax.random.fold_in(stream_key, 1), (couples,), 0, 1 << 20) % (room + 1)
    lengths = lengths.at[1:1 + 2 * couples:2].set(giver - shifted).at[2:2 + 2 * couples:2].set(taker + shifted)
    return lengths[jax.random.permutation(jax.random.fold_in(stream_key, 2), count)]


def centred(rng, extent, width, most, split=(), held_as=jnp.bfloat16):
    level = levels(rng, extent, split, -0.22, 0.18) if split else 1.0
    entries = jax.random.normal(rng, extent, jnp.float32) * width * level
    return jnp.minimum(jnp.maximum(entries, -most), most).astype(held_as)


def setup_inputs(seed: int = 0) -> dict:
    key_list = jax.random.split(jax.random.key(seed), 6)
    return {
        "queries": draw_queries(jax.random.fold_in(key_list[5], 71), 0),
        "keys_in": draw_keys_in(jax.random.fold_in(key_list[5], 71), 0),
        "values": centred(key_list[2], (TOKENS, HEADS * HEAD_DIM), 1.0, 6.0, ((0, 128),)),
        "out_grad": centred(key_list[3], (TOKENS, HEADS * HEAD_DIM), 1.0, 6.0, ((0, 128),)),
        "doc_lengths": uneven(key_list[4], NDOCS, TOKENS, MAXDOC, 2).astype(jnp.int32),
    }


masked_value = -1e30


def reference(queries, keys_in, values, out_grad, doc_lengths):
    row_length = queries.shape[0]
    all_heads = queries.shape[1] // HEAD_DIM
    margin = REACH * TOK_DEV
    window = (2 * REACH + 1) * TOK_DEV
    score_scale = HEAD_DIM ** -0.5
    doc_ends = jnp.cumsum(doc_lengths).astype(jnp.int32)
    position = jnp.arange(row_length, dtype=jnp.int32)
    doc_index = jnp.sum((position[:, None] >= doc_ends[None, :]).astype(jnp.int32), axis=1).astype(jnp.int32)
    padded_docs = jnp.pad(doc_index, (margin, margin), constant_values=-2)

    def heads_of(matrix):
        return matrix.reshape(row_length, all_heads, HEAD_DIM).astype(jnp.float32)

    query_heads = heads_of(queries)
    key_heads = heads_of(keys_in)
    value_heads = heads_of(values)
    grad_heads = heads_of(out_grad)
    widths = ((margin, margin), (0, 0), (0, 0))
    key_padded = jnp.pad(key_heads, widths)
    value_padded = jnp.pad(value_heads, widths)

    def one_block(carry, block_index):
        key_total, value_total = carry
        start = (block_index * TOK_DEV).astype(jnp.int32)
        query_block = lax.dynamic_slice_in_dim(query_heads, start, TOK_DEV, 0)
        grad_block = lax.dynamic_slice_in_dim(grad_heads, start, TOK_DEV, 0)
        own_docs = lax.dynamic_slice_in_dim(doc_index, start, TOK_DEV, 0)
        key_window = lax.dynamic_slice_in_dim(key_padded, start, window, 0)
        value_window = lax.dynamic_slice_in_dim(value_padded, start, window, 0)
        window_docs = lax.dynamic_slice_in_dim(padded_docs, start, window, 0)
        allowed = (own_docs[:, None] == window_docs[None, :])[None]
        scores = jnp.einsum("qhd,khd->hqk", query_block, key_window) * score_scale
        masked = jnp.where(allowed, scores, masked_value)
        row_peak = jnp.max(masked, axis=-1)
        row_mass = jnp.sum(jnp.where(allowed, jnp.exp(masked - row_peak[..., None]), 0.0), axis=-1)
        log_norm = row_peak + jnp.log(row_mass)
        probs = jnp.where(allowed, jnp.exp(scores - log_norm[..., None]), 0.0)
        probs_low = lax.optimization_barrier(probs.astype(jnp.bfloat16)).astype(jnp.float32)
        output = jnp.einsum("hqk,khd->qhd", probs_low, value_window).astype(jnp.bfloat16)
        row_dot = jnp.sum(grad_block * output.astype(jnp.float32), axis=-1).T
        dprob = jnp.einsum("qhd,khd->hqk", grad_block, value_window)
        dscore = lax.optimization_barrier((probs * (dprob - row_dot[..., None])).astype(jnp.bfloat16)).astype(jnp.float32)
        query_part = (jnp.einsum("hqk,khd->qhd", dscore, key_window) * score_scale).astype(jnp.bfloat16)
        key_part = jnp.einsum("hqk,qhd->khd", dscore, query_block)
        value_part = jnp.einsum("hqk,qhd->khd", probs_low, grad_block)
        key_total = lax.dynamic_update_slice_in_dim(key_total, lax.dynamic_slice_in_dim(key_total, start, window, 0) + key_part, start, 0)
        value_total = lax.dynamic_update_slice_in_dim(value_total, lax.dynamic_slice_in_dim(value_total, start, window, 0) + value_part, start, 0)
        return (key_total, value_total), (output, query_part)

    zeros = jnp.zeros((row_length + 2 * margin, all_heads, HEAD_DIM), jnp.float32)
    blocks = jnp.arange(row_length // TOK_DEV, dtype=jnp.int32)
    (key_total, value_total), (output, query_part) = lax.scan(one_block, (zeros, zeros), blocks)
    flat = (row_length, all_heads * HEAD_DIM)
    key_grad = (key_total[margin:margin + row_length] * score_scale).astype(jnp.bfloat16).reshape(flat)
    value_grad = value_total[margin:margin + row_length].astype(jnp.bfloat16).reshape(flat)
    return (output.reshape(flat), query_part.reshape(flat), key_grad, value_grad)
```

```python
import functools

import jax
import jax.numpy as jnp
from jax import lax
from jax.experimental import pallas as pl
from jax.experimental.pallas import tpu as pltpu
from jax.sharding import PartitionSpec as P

HEAD_DIM = 128
NDOCS = 15
GROUP = 2048
PIECE = 128
PIECES = GROUP // PIECE
QT = 256
KT = 512
UNIT = 256
WINDOW = 3 * GROUP
PADDED = WINDOW + KT
SPAN = 9 * KT
TOKENS = 16384
MASK = 1024.0
SCALE = HEAD_DIM ** (-0.5)
LOG2E = 1.4426950408889634
MESH = pl.DeviceIdType.MESH
BF = jnp.bfloat16
F32 = jnp.float32


def place():
    ctx = lax.axis_index("ctx")
    y = lax.axis_index("head")
    x = ctx // 8
    z = (ctx // 2) % 4
    core = ctx % 2
    return x, z, core, y


def ctx_of(x, z, core):
    return (x * 4 + z) * 2 + core


def x_partner(x, core):
    return jnp.where(core == 0, (x + 3) % 4, (x + 1) % 4)


def gather_kernel(q_in, k_in, v_in, g_in, q_out, g_out, k_out, v_out, send, recv, hsend, hrecv):
    x, z, core, y = place()
    my_slot = ((2 * z + core) % 4) * 4 + y
    half = z // 2
    sibling = {"ctx": ctx_of(x, z, 1 - core), "head": y}
    beside = {"ctx": ctx_of(x_partner(x, core), z, 1 - core), "head": y}
    barrier = pltpu.get_barrier_semaphore()

    def is_self(zz, cc, yy):
        return (zz == z) & (cc == core) & (yy == y)

    def greet(s, c):
        zz = 2 * core + s // 8
        cc = (s // 4) % 2
        yy = s % 4

        @pl.when(jnp.logical_not(is_self(zz, cc, yy)))
        def _():
            pl.semaphore_signal(
                barrier, inc=1, device_id={"ctx": ctx_of(x, zz, cc), "head": yy}, device_id_type=MESH
            )

        return c

    lax.fori_loop(0, PIECES, greet, 0)
    pl.semaphore_signal(barrier, inc=1, device_id=sibling, device_id_type=MESH)
    pl.semaphore_signal(barrier, inc=1, device_id=beside, device_id_type=MESH)
    pl.semaphore_wait(barrier, jnp.where(half == core, PIECES - 1, PIECES) + 2)

    arrays = ((0, k_in, k_out), (1, v_in, v_out), (2, q_in, q_out), (3, g_in, g_out))

    def target(out, a):
        return out.at[1] if a < 2 else out

    def remote(a, src, out, step):
        zz = (z + step // 4) % 4
        yy = (y + step % 4) % 4
        head = zz * 4 + yy
        return (
            zz,
            yy,
            src.at[:, pl.ds(pl.multiple_of(head * HEAD_DIM, HEAD_DIM), HEAD_DIM)],
            target(out, a).at[pl.ds(pl.multiple_of(my_slot * PIECE, PIECE), PIECE), :],
        )

    def remote_copy(a, src, out, step):
        zz, yy, s_ref, d_ref = remote(a, src, out, step)
        return pltpu.make_async_remote_copy(
            src_ref=s_ref,
            dst_ref=d_ref,
            send_sem=send.at[a, step],
            recv_sem=recv.at[a, my_slot],
            device_id={"ctx": ctx_of(x, zz, half), "head": yy},
            device_id_type=MESH,
        )

    for a, src, out in arrays:

        @pl.when(half == core)
        def _():
            _, _, s_ref, d_ref = remote(a, src, out, 0)
            pltpu.make_async_copy(s_ref, d_ref, recv.at[a, my_slot]).start()

        @pl.when(half != core)
        def _():
            remote_copy(a, src, out, 0).start()

        def start(step, c):
            remote_copy(a, src, out, step).start()
            return c

        lax.fori_loop(1, PIECES, start, 0)

    def wait_all(a, out):
        def wait(s, c):
            piece = target(out, a).at[pl.ds(pl.multiple_of(s * PIECE, PIECE), PIECE), :]
            pltpu.make_async_copy(piece, piece, recv.at[a, s]).wait()
            return c

        lax.fori_loop(0, PIECES, wait, 0)

    halos = []
    for a, src, out in arrays[:2]:
        wait_all(a, out)
        sib = pltpu.make_async_remote_copy(
            src_ref=out.at[1],
            dst_ref=out.at[2 * core],
            send_sem=hsend.at[a, 0],
            recv_sem=hrecv.at[a, 0],
            device_id=sibling,
            device_id_type=MESH,
        )
        far = pltpu.make_async_remote_copy(
            src_ref=out.at[1],
            dst_ref=out.at[2 * (1 - core)],
            send_sem=hsend.at[a, 1],
            recv_sem=hrecv.at[a, 1],
            device_id=beside,
            device_id_type=MESH,
        )
        far.start()
        sib.start()
        halos += [sib, far]
    for a, src, out in arrays[2:]:
        wait_all(a, out)
    for copy in halos:
        copy.wait()
    for a, src, out in arrays:

        @pl.when(half != core)
        def _():
            remote_copy(a, src, out, 0).wait_send()

        def wait_sent(step, c):
            remote_copy(a, src, out, step).wait_send()
            return c

        lax.fori_loop(1, PIECES, wait_sent, 0)


def gather(q, k, v, g):
    any_spec = pl.BlockSpec(memory_space=pl.ANY)
    own = jax.ShapeDtypeStruct((GROUP, HEAD_DIM), BF)
    window = jax.ShapeDtypeStruct((3, GROUP, HEAD_DIM), BF)
    return pl.pallas_call(
        gather_kernel,
        out_shape=(own, own, window, window),
        in_specs=[any_spec] * 4,
        out_specs=(any_spec,) * 4,
        scratch_shapes=[
            pltpu.SemaphoreType.DMA((4, PIECES)),
            pltpu.SemaphoreType.DMA((4, PIECES)),
            pltpu.SemaphoreType.DMA((2, 2)),
            pltpu.SemaphoreType.DMA((2, 2)),
        ],
        compiler_params=pltpu.CompilerParams(collective_id=0, has_side_effects=True),
        name="to_heads",
    )(q, k, v, g)


def dot_nt(a, b):
    return lax.dot_general(a, b, (((1,), (1,)), ((), ())), preferred_element_type=F32)


def dot_nn(a, b):
    return lax.dot_general(a, b, (((1,), (0,)), ((), ())), preferred_element_type=F32)


def attend_kernel(
    lens, q_ref, g_ref, kw, vw, att_ref, dq_ref, own_ref, side_ref,
    ke, ve, s_scr, p_scr, o_acc, dq_acc, dk_acc, dv_acc,
):
    ctx = lax.axis_index("ctx")
    group = (ctx // 8) * 2 + ctx % 2
    base = (group - 1) * GROUP
    lane = lax.broadcasted_iota(jnp.int32, (1, 128), 1)
    starts = jnp.full((1, 128), 1 << 30, jnp.int32)
    ends = jnp.full((1, 128), 1 << 30, jnp.int32)
    bounds = [jnp.int32(0)]
    for j in range(NDOCS):
        starts = jnp.where(lane == j, bounds[-1], starts)
        bounds.append(bounds[-1] + lens[j])
        ends = jnp.where(lane == j, bounds[-1], ends)
    starts = jnp.where(lane == 127, TOKENS, jnp.where(lane == 126, -(1 << 30), starts))
    ends = jnp.where(lane == 126, 0, ends)
    row = lax.broadcasted_iota(jnp.int32, (QT, 128), 0)

    def in_doc(first):
        pos = first + row
        return (pos >= starts) & (pos < ends)

    ones = jnp.ones((QT, 128), BF)

    def build(b, c):
        rows = pl.ds(pl.multiple_of(b * QT, QT), QT)
        flag = jnp.where(in_doc(base + b * QT), -MASK, 0.0).astype(BF)
        ke[rows, :] = jnp.concatenate([kw[rows, :], flag], axis=1)
        ve[rows, :] = jnp.concatenate([vw[rows, :], ones], axis=1)
        return c

    lax.fori_loop(0, WINDOW // QT, build, 0)
    for b in range(WINDOW // QT, PADDED // QT):
        rows = pl.ds(b * QT, QT)
        flag = jnp.where(in_doc(base + b * QT), -MASK, 0.0).astype(BF)
        ke[rows, :] = jnp.concatenate([jnp.zeros((QT, 128), BF), flag], axis=1)
        ve[rows, :] = jnp.zeros((QT, 256), BF)
    dk_acc[...] = jnp.zeros_like(dk_acc)
    dv_acc[...] = jnp.zeros_like(dv_acc)

    lane_tile = lax.broadcasted_iota(jnp.int32, (QT, 128), 1)

    def query_tile(i, c):
        rows = pl.ds(pl.multiple_of(i * QT, QT), QT)
        r0 = group * GROUP + i * QT
        lo = jnp.int32(0)
        hi = jnp.int32(TOKENS)
        for e in bounds[1:]:
            lo = jnp.where(e <= r0, jnp.maximum(lo, e), lo)
            hi = jnp.where(e > r0 + (QT - 1), jnp.minimum(hi, e), hi)
        first = (lo - base) // UNIT
        steps = (hi - base - first * UNIT + (KT - 1)) // KT

        q = q_ref[rows, :]
        g = g_ref[rows, :]
        qe = jnp.concatenate([q, jnp.where(in_doc(r0), 0.0, MASK).astype(BF)], axis=1)

        def krows(t):
            return pl.ds(pl.multiple_of(first * UNIT + t * KT, UNIT), KT)

        def score_step(t, peak):
            s = dot_nt(qe, ke[krows(t), :])
            s_scr[t] = s
            for j in range(KT // 128):
                peak = jnp.maximum(peak, s[:, j * 128:(j + 1) * 128])
            return peak

        peak = lax.fori_loop(0, steps, score_step, jnp.full((QT, 128), -3e38, F32))
        peak = jnp.max(peak, axis=1, keepdims=True)

        o_acc[...] = jnp.zeros_like(o_acc)

        def prob_step(t, c):
            p = jnp.exp2((s_scr[t] - peak) * (SCALE * LOG2E)).astype(BF)
            p_scr[t] = p
            o_acc[...] += dot_nn(p, ve[krows(t), :])
            return c

        lax.fori_loop(0, steps, prob_step, 0)
        inv = 1.0 / o_acc[:, 128:]
        att = (o_acc[:, :128] * inv).astype(BF)
        att_ref[rows, :] = att
        g32 = g.astype(F32)
        neg = -jnp.sum(g32 * att.astype(F32), axis=1, keepdims=True)
        n0 = neg.astype(BF).astype(F32)
        n1 = (neg - n0).astype(BF).astype(F32)
        n2 = neg - n0 - n1
        extra = jnp.where(
            lane_tile == 0, n0, jnp.where(lane_tile == 1, n1, jnp.where(lane_tile == 2, n2, 0.0))
        ).astype(BF)
        ge = jnp.concatenate([g, extra], axis=1)
        gt = (g32 * inv).T.astype(BF)
        qt = (q.astype(F32) * (inv * SCALE)).T.astype(BF)
        dq_acc[...] = jnp.zeros_like(dq_acc)

        def grad_step(t, c):
            keys = krows(t)
            p = p_scr[t]
            dp = dot_nt(ge, ve[keys, :])
            ds = (p.astype(F32) * dp).astype(BF)
            dq_acc[...] += dot_nn(ds, ke[keys, :128])
            dk_acc[:, keys] += dot_nn(qt, ds)
            dv_acc[:, keys] += dot_nn(gt, p)
            return c

        lax.fori_loop(0, steps, grad_step, 0)
        dq_ref[rows, :] = (dq_acc[...] * (inv * SCALE)).astype(BF)
        return c

    lax.fori_loop(0, GROUP // QT, query_tile, 0)
    for a, acc in ((0, dk_acc), (1, dv_acc)):
        own_ref[a] = acc[:, GROUP:2 * GROUP]
        side_ref[a, 0] = acc[:, :GROUP].astype(BF)
        side_ref[a, 1] = acc[:, 2 * GROUP:3 * GROUP].astype(BF)


def attend(lens, q, g, kw, vw):
    vmem = pl.BlockSpec(memory_space=pltpu.VMEM)
    own = jax.ShapeDtypeStruct((GROUP, HEAD_DIM), BF)
    return pl.pallas_call(
        attend_kernel,
        out_shape=(
            own,
            own,
            jax.ShapeDtypeStruct((2, HEAD_DIM, GROUP), F32),
            jax.ShapeDtypeStruct((2, 2, HEAD_DIM, GROUP), BF),
        ),
        in_specs=[pl.BlockSpec(memory_space=pltpu.SMEM)] + [vmem] * 4,
        out_specs=(vmem,) * 4,
        scratch_shapes=[
            pltpu.VMEM((PADDED, 256), BF),
            pltpu.VMEM((PADDED, 256), BF),
            pltpu.VMEM((SPAN // KT, QT, KT), F32),
            pltpu.VMEM((SPAN // KT, QT, KT), BF),
            pltpu.VMEM((QT, 256), F32),
            pltpu.VMEM((QT, 128), F32),
            pltpu.VMEM((128, PADDED), F32),
            pltpu.VMEM((128, PADDED), F32),
        ],
        compiler_params=pltpu.CompilerParams(vmem_limit_bytes=56 * 1024 * 1024),
        name="attend",
    )(lens, q, g, kw.reshape(WINDOW, HEAD_DIM), vw.reshape(WINDOW, HEAD_DIM))


def scatter_kernel(
    att, dq, own, side, att_out, dq_out, dk_out, dv_out, halo, total, send, recv, hsend, hrecv
):
    x, z, core, y = place()
    my_slot = ((2 * z + core) % 4) * 4 + y
    head = z * 4 + y
    half = z // 2
    sibling = {"ctx": ctx_of(x, z, 1 - core), "head": y}
    beside = {"ctx": ctx_of(x_partner(x, core), z, 1 - core), "head": y}
    barrier = pltpu.get_barrier_semaphore()

    def greet(step, c):
        zz = (z + step // 4) % 4
        yy = (y + step % 4) % 4

        @pl.when((step > 0) | (half != core))
        def _():
            pl.semaphore_signal(
                barrier, inc=1, device_id={"ctx": ctx_of(x, zz, half), "head": yy}, device_id_type=MESH
            )

        return c

    lax.fori_loop(0, PIECES, greet, 0)
    pl.semaphore_signal(barrier, inc=1, device_id=sibling, device_id_type=MESH)
    pl.semaphore_signal(barrier, inc=1, device_id=beside, device_id_type=MESH)
    pl.semaphore_wait(barrier, jnp.where(half == core, PIECES - 1, PIECES) + 2)

    halos = []
    for a in range(2):
        halos.append(
            pltpu.make_async_remote_copy(
                src_ref=side.at[a, core],
                dst_ref=halo.at[a, 1],
                send_sem=hsend.at[a, 1],
                recv_sem=hrecv.at[a, 1],
                device_id=beside,
                device_id_type=MESH,
            )
        )
        halos.append(
            pltpu.make_async_remote_copy(
                src_ref=side.at[a, 1 - core],
                dst_ref=halo.at[a, 0],
                send_sem=hsend.at[a, 0],
                recv_sem=hrecv.at[a, 0],
                device_id=sibling,
                device_id_type=MESH,
            )
        )
    for copy in halos:
        copy.start()

    outs = (att_out, dq_out, dk_out, dv_out)
    srcs = (att, dq, total.at[0], total.at[1])

    def columns(h):
        return pl.ds(pl.multiple_of(h * HEAD_DIM, HEAD_DIM), HEAD_DIM)

    def slot_of(step):
        return (my_slot + step) % PIECES

    def place_of(s):
        return 2 * core + s // 8, (s // 4) % 2, s % 4

    def local(s):
        zz, cc, yy = place_of(s)
        return (zz == z) & (cc == core) & (yy == y)

    def piece(a, s):
        return srcs[a].at[pl.ds(pl.multiple_of(s * PIECE, PIECE), PIECE), :]

    def remote_copy(a, s):
        zz, cc, yy = place_of(s)
        return pltpu.make_async_remote_copy(
            src_ref=piece(a, s),
            dst_ref=outs[a].at[:, columns(head)],
            send_sem=send.at[a, s],
            recv_sem=recv.at[a, head],
            device_id={"ctx": ctx_of(x, zz, cc), "head": yy},
            device_id_type=MESH,
        )

    def send_all(a):
        def start(step, c):
            s = slot_of(step)
            mine = local(s)

            @pl.when(mine)
            def _():
                pltpu.make_async_copy(
                    piece(a, s), outs[a].at[:, columns(head)], recv.at[a, head]
                ).start()

            @pl.when(jnp.logical_not(mine))
            def _():
                remote_copy(a, s).start()

            return c

        lax.fori_loop(0, PIECES, start, 0)

    send_all(0)
    send_all(1)
    for a in range(2):
        halos[2 * a].wait_recv()
        halos[2 * a + 1].wait_recv()

        def sum_piece(s, c):
            cols = pl.ds(pl.multiple_of(s * PIECE, PIECE), PIECE)
            tot = (
                own[a, :, cols]
                + halo[a, 0, :, cols].astype(F32)
                + halo[a, 1, :, cols].astype(F32)
            )
            total[a, cols, :] = tot.T.astype(BF)
            return c

        lax.fori_loop(0, PIECES, sum_piece, 0)
        send_all(2 + a)
    for copy in halos:
        copy.wait_send()
    for a in range(4):

        def wait(h, c):
            part = outs[a].at[:, columns(h)]
            pltpu.make_async_copy(part, part, recv.at[a, h]).wait()

            @pl.when(jnp.logical_not(local(h)))
            def _():
                remote_copy(a, h).wait_send()

            return c

        lax.fori_loop(0, PIECES, wait, 0)


def scatter(att, dq, own, side):
    any_spec = pl.BlockSpec(memory_space=pl.ANY)
    out = jax.ShapeDtypeStruct((PIECE, PIECES * HEAD_DIM), BF)
    return pl.pallas_call(
        scatter_kernel,
        out_shape=(out,) * 4,
        in_specs=[any_spec, any_spec, pl.BlockSpec(memory_space=pltpu.VMEM), any_spec],
        out_specs=(any_spec,) * 4,
        scratch_shapes=[
            pltpu.VMEM((2, 2, HEAD_DIM, GROUP), BF),
            pltpu.VMEM((2, GROUP, HEAD_DIM), BF),
            pltpu.SemaphoreType.DMA((4, PIECES)),
            pltpu.SemaphoreType.DMA((4, PIECES)),
            pltpu.SemaphoreType.DMA((2, 2)),
            pltpu.SemaphoreType.DMA((2, 2)),
        ],
        compiler_params=pltpu.CompilerParams(
            collective_id=1, has_side_effects=True, vmem_limit_bytes=32 * 1024 * 1024
        ),
        name="to_tokens",
    )(att, dq, own, side)


def body(queries, keys_in, values, out_grad, doc_lengths):
    q, g, kw, vw = gather(queries, keys_in, values, out_grad)
    att, dq, own, side = attend(doc_lengths, q, g, kw, vw)
    return scatter(att, dq, own, side)


def solution(mesh):
    tokens = P(("ctx", "head"), None)
    return jax.shard_map(
        body,
        mesh=mesh,
        in_specs=(tokens,) * 4 + (P(),),
        out_specs=(tokens,) * 4,
        check_vma=False,
    )
```

```python
import functools

import jax
import jax.numpy as jnp
from jax import lax
from jax.experimental import pallas as pl
from jax.experimental.pallas import tpu as pltpu
from jax.sharding import PartitionSpec as P

HEAD_DIM = 128
NDOCS = 15
GROUP = 2048
PIECE = 128
PIECES = GROUP // PIECE
QT = 256
KT = 2304
UNIT = 128
WINDOW = 3 * GROUP
BT = 256
STEPS = -(-(2 * GROUP + QT + UNIT) // KT)
TOKENS = 16384
MASK = 1024.0
SCALE = HEAD_DIM ** (-0.5)
LOG2E = 1.4426950408889634
MESH = pl.DeviceIdType.MESH
BF = jnp.bfloat16
F32 = jnp.float32


def place():
    ctx = lax.axis_index("ctx")
    y = lax.axis_index("head")
    x = ctx // 8
    z = (ctx // 2) % 4
    core = ctx % 2
    return x, z, core, y


def ctx_of(x, z, core):
    return (x * 4 + z) * 2 + core


def x_partner(x, core):
    return jnp.where(core == 0, (x + 3) % 4, (x + 1) % 4)


def gather_kernel(q_in, k_in, v_in, g_in, q_out, g_out, k_out, v_out, send, recv, hsend, hrecv):
    x, z, core, y = place()
    my_slot = ((2 * z + core) % 4) * 4 + y
    half = z // 2
    sibling = {"ctx": ctx_of(x, z, 1 - core), "head": y}
    beside = {"ctx": ctx_of(x_partner(x, core), z, 1 - core), "head": y}
    barrier = pltpu.get_barrier_semaphore()

    def is_self(zz, cc, yy):
        return (zz == z) & (cc == core) & (yy == y)

    def greet(s, c):
        zz = 2 * core + s // 8
        cc = (s // 4) % 2
        yy = s % 4

        @pl.when(jnp.logical_not(is_self(zz, cc, yy)))
        def _():
            pl.semaphore_signal(
                barrier, inc=1, device_id={"ctx": ctx_of(x, zz, cc), "head": yy}, device_id_type=MESH
            )

        return c

    lax.fori_loop(0, PIECES, greet, 0)
    pl.semaphore_signal(barrier, inc=1, device_id=sibling, device_id_type=MESH)
    pl.semaphore_signal(barrier, inc=1, device_id=beside, device_id_type=MESH)
    pl.semaphore_wait(barrier, jnp.where(half == core, PIECES - 1, PIECES) + 2)

    arrays = ((0, k_in, k_out), (1, v_in, v_out), (2, q_in, q_out), (3, g_in, g_out))

    def target(out, a):
        return out.at[1] if a < 2 else out

    def remote(a, src, out, step):
        zz = (z + step // 4) % 4
        yy = (y + step % 4) % 4
        head = zz * 4 + yy
        return (
            zz,
            yy,
            src.at[:, pl.ds(pl.multiple_of(head * HEAD_DIM, HEAD_DIM), HEAD_DIM)],
            target(out, a).at[pl.ds(pl.multiple_of(my_slot * PIECE, PIECE), PIECE), :],
        )

    def remote_copy(a, src, out, step):
        zz, yy, s_ref, d_ref = remote(a, src, out, step)
        return pltpu.make_async_remote_copy(
            src_ref=s_ref,
            dst_ref=d_ref,
            send_sem=send.at[a, step],
            recv_sem=recv.at[a, my_slot],
            device_id={"ctx": ctx_of(x, zz, half), "head": yy},
            device_id_type=MESH,
        )

    for a, src, out in arrays:

        @pl.when(half == core)
        def _():
            _, _, s_ref, d_ref = remote(a, src, out, 0)
            pltpu.make_async_copy(s_ref, d_ref, recv.at[a, my_slot]).start()

        @pl.when(half != core)
        def _():
            remote_copy(a, src, out, 0).start()

        def start(step, c):
            remote_copy(a, src, out, step).start()
            return c

        lax.fori_loop(1, PIECES, start, 0)

    def wait_all(a, out):
        def wait(s, c):
            piece = target(out, a).at[pl.ds(pl.multiple_of(s * PIECE, PIECE), PIECE), :]
            pltpu.make_async_copy(piece, piece, recv.at[a, s]).wait()
            return c

        lax.fori_loop(0, PIECES, wait, 0)

    halos = []
    for a, src, out in arrays[:2]:
        wait_all(a, out)
        sib = pltpu.make_async_remote_copy(
            src_ref=out.at[1],
            dst_ref=out.at[2 * core],
            send_sem=hsend.at[a, 0],
            recv_sem=hrecv.at[a, 0],
            device_id=sibling,
            device_id_type=MESH,
        )
        far = pltpu.make_async_remote_copy(
            src_ref=out.at[1],
            dst_ref=out.at[2 * (1 - core)],
            send_sem=hsend.at[a, 1],
            recv_sem=hrecv.at[a, 1],
            device_id=beside,
            device_id_type=MESH,
        )
        far.start()
        sib.start()
        halos += [sib, far]
    for a, src, out in arrays[2:]:
        wait_all(a, out)
    for copy in halos:
        copy.wait()
    for a, src, out in arrays:

        @pl.when(half != core)
        def _():
            remote_copy(a, src, out, 0).wait_send()

        def wait_sent(step, c):
            remote_copy(a, src, out, step).wait_send()
            return c

        lax.fori_loop(1, PIECES, wait_sent, 0)


def gather(q, k, v, g):
    any_spec = pl.BlockSpec(memory_space=pl.ANY)
    own = jax.ShapeDtypeStruct((GROUP, HEAD_DIM), BF)
    window = jax.ShapeDtypeStruct((3, GROUP, HEAD_DIM), BF)
    return pl.pallas_call(
        gather_kernel,
        out_shape=(own, own, window, window),
        in_specs=[any_spec] * 4,
        out_specs=(any_spec,) * 4,
        scratch_shapes=[
            pltpu.SemaphoreType.DMA((4, PIECES)),
            pltpu.SemaphoreType.DMA((4, PIECES)),
            pltpu.SemaphoreType.DMA((2, 2)),
            pltpu.SemaphoreType.DMA((2, 2)),
        ],
        compiler_params=pltpu.CompilerParams(collective_id=0, has_side_effects=True),
        name="to_heads",
    )(q, k, v, g)


def dot_nt(a, b):
    return lax.dot_general(a, b, (((1,), (1,)), ((), ())), preferred_element_type=F32)


def dot_nn(a, b):
    return lax.dot_general(a, b, (((1,), (0,)), ((), ())), preferred_element_type=F32)


def attend_kernel(
    lens, q_ref, g_ref, kw, vw, att_ref, dq_ref, own_ref, side_ref,
    ke, ve, s_scr, p_scr, o_acc, dq_acc, dk_acc, dv_acc,
):
    ctx = lax.axis_index("ctx")
    group = (ctx // 8) * 2 + ctx % 2
    base = (group - 1) * GROUP
    lane = lax.broadcasted_iota(jnp.int32, (1, 128), 1)
    starts = jnp.full((1, 128), 1 << 30, jnp.int32)
    ends = jnp.full((1, 128), 1 << 30, jnp.int32)
    bounds = [jnp.int32(0)]
    for j in range(NDOCS):
        starts = jnp.where(lane == j, bounds[-1], starts)
        bounds.append(bounds[-1] + lens[j])
        ends = jnp.where(lane == j, bounds[-1], ends)
    starts = jnp.where(lane == 127, TOKENS, jnp.where(lane == 126, -(1 << 30), starts))
    ends = jnp.where(lane == 126, 0, ends)

    def in_doc(first, count):
        pos = first + lax.broadcasted_iota(jnp.int32, (count, 128), 0)
        return (pos >= starts) & (pos < ends)

    ones = jnp.ones((BT, 128), BF)

    def build(b, c):
        rows = pl.ds(pl.multiple_of(b * BT, BT), BT)
        flag = jnp.where(in_doc(base + b * BT, BT), -MASK, 0.0).astype(BF)
        ke[rows, :] = jnp.concatenate([kw[rows, :], flag], axis=1)
        ve[rows, :] = jnp.concatenate([vw[rows, :], ones], axis=1)
        return c

    lax.fori_loop(0, WINDOW // BT, build, 0)
    dk_acc[...] = jnp.zeros_like(dk_acc)
    dv_acc[...] = jnp.zeros_like(dv_acc)

    lane_tile = lax.broadcasted_iota(jnp.int32, (QT, 128), 1)

    def query_tile(i, c):
        rows = pl.ds(pl.multiple_of(i * QT, QT), QT)
        r0 = group * GROUP + i * QT
        lo = jnp.int32(0)
        hi = jnp.int32(TOKENS)
        for e in bounds[1:]:
            lo = jnp.where(e <= r0, jnp.maximum(lo, e), lo)
            hi = jnp.where(e > r0 + (QT - 1), jnp.minimum(hi, e), hi)
        first = (lo - base) // UNIT
        steps = (hi - base - first * UNIT + (KT - 1)) // KT
        first = jnp.minimum(first, (WINDOW - steps * KT) // UNIT)

        q = q_ref[rows, :]
        g = g_ref[rows, :]
        qe = jnp.concatenate([q, jnp.where(in_doc(r0, QT), 0.0, MASK).astype(BF)], axis=1)

        def krows(t, j=0, n=KT):
            return pl.ds(pl.multiple_of(first * UNIT + t * KT + j, UNIT), n)

        def score_step(t, peak):
            for o in range(0, KT, KT):
                s = dot_nt(qe, ke[krows(t, o, KT), :])
                s_scr[t, :, o:o + KT] = s
                for j in range(KT // 128):
                    peak = jnp.maximum(peak, s[:, j * 128:(j + 1) * 128])
            return peak

        peak = lax.fori_loop(0, steps, score_step, jnp.full((QT, 128), -3e38, F32))
        peak = jnp.max(peak, axis=1, keepdims=True)

        o_acc[...] = jnp.zeros_like(o_acc)

        def prob_step(t, c):
            tot = o_acc[...]
            for o in range(0, KT, KT):
                p = jnp.exp2((s_scr[t, :, o:o + KT] - peak) * (SCALE * LOG2E)).astype(BF)
                p_scr[t, :, o:o + KT] = p
                tot += dot_nn(p, ve[krows(t, o, KT), :])
            o_acc[...] = tot
            return c

        lax.fori_loop(0, steps, prob_step, 0)
        inv = 1.0 / o_acc[:, 128:]
        att = (o_acc[:, :128] * inv).astype(BF)
        att_ref[rows, :] = att
        g32 = g.astype(F32)
        neg = -jnp.sum(g32 * att.astype(F32), axis=1, keepdims=True)
        n0 = neg.astype(BF).astype(F32)
        n1 = (neg - n0).astype(BF).astype(F32)
        n2 = neg - n0 - n1
        extra = jnp.where(
            lane_tile == 0, n0, jnp.where(lane_tile == 1, n1, jnp.where(lane_tile == 2, n2, 0.0))
        ).astype(BF)
        ge = jnp.concatenate([g, extra], axis=1)
        gt = (g32 * inv).T.astype(BF)
        qt = (q.astype(F32) * (inv * SCALE)).T.astype(BF)
        dq_acc[...] = jnp.zeros_like(dq_acc)

        def grad_step(t, c):
            tot = dq_acc[...]
            for o in range(0, KT, KT):
                keys = krows(t, o, KT)
                p = p_scr[t, :, o:o + KT]
                dp = dot_nt(ge, ve[keys, :])
                ds = (p.astype(F32) * dp).astype(BF)
                tot += dot_nn(ds, ke[keys, :128])
                dk_acc[:, keys] += dot_nn(qt, ds)
                dv_acc[:, keys] += dot_nn(gt, p)
            dq_acc[...] = tot
            return c

        lax.fori_loop(0, steps, grad_step, 0)
        dq_ref[rows, :] = (dq_acc[...] * (inv * SCALE)).astype(BF)
        return c

    lax.fori_loop(0, GROUP // QT, query_tile, 0)
    for a, acc in ((0, dk_acc), (1, dv_acc)):
        own_ref[a] = acc[:, GROUP:2 * GROUP]
        side_ref[a, 0] = acc[:, :GROUP].astype(BF)
        side_ref[a, 1] = acc[:, 2 * GROUP:3 * GROUP].astype(BF)


def attend(lens, q, g, kw, vw):
    vmem = pl.BlockSpec(memory_space=pltpu.VMEM)
    own = jax.ShapeDtypeStruct((GROUP, HEAD_DIM), BF)
    return pl.pallas_call(
        attend_kernel,
        out_shape=(
            own,
            own,
            jax.ShapeDtypeStruct((2, HEAD_DIM, GROUP), F32),
            jax.ShapeDtypeStruct((2, 2, HEAD_DIM, GROUP), BF),
        ),
        in_specs=[pl.BlockSpec(memory_space=pltpu.SMEM)] + [vmem] * 4,
        out_specs=(vmem,) * 4,
        scratch_shapes=[
            pltpu.VMEM((WINDOW, 256), BF),
            pltpu.VMEM((WINDOW, 256), BF),
            pltpu.VMEM((STEPS, QT, KT), F32),
            pltpu.VMEM((STEPS, QT, KT), BF),
            pltpu.VMEM((QT, 256), F32),
            pltpu.VMEM((QT, 128), F32),
            pltpu.VMEM((128, WINDOW), F32),
            pltpu.VMEM((128, WINDOW), F32),
        ],
        compiler_params=pltpu.CompilerParams(vmem_limit_bytes=56 * 1024 * 1024),
        name="attend",
    )(lens, q, g, kw.reshape(WINDOW, HEAD_DIM), vw.reshape(WINDOW, HEAD_DIM))


def scatter_kernel(
    att, dq, own, side, att_out, dq_out, dk_out, dv_out, halo, total, send, recv, hsend, hrecv
):
    x, z, core, y = place()
    my_slot = ((2 * z + core) % 4) * 4 + y
    head = z * 4 + y
    half = z // 2
    sibling = {"ctx": ctx_of(x, z, 1 - core), "head": y}
    beside = {"ctx": ctx_of(x_partner(x, core), z, 1 - core), "head": y}
    barrier = pltpu.get_barrier_semaphore()

    def greet(step, c):
        zz = (z + step // 4) % 4
        yy = (y + step % 4) % 4

        @pl.when((step > 0) | (half != core))
        def _():
            pl.semaphore_signal(
                barrier, inc=1, device_id={"ctx": ctx_of(x, zz, half), "head": yy}, device_id_type=MESH
            )

        return c

    lax.fori_loop(0, PIECES, greet, 0)
    pl.semaphore_signal(barrier, inc=1, device_id=sibling, device_id_type=MESH)
    pl.semaphore_signal(barrier, inc=1, device_id=beside, device_id_type=MESH)
    pl.semaphore_wait(barrier, jnp.where(half == core, PIECES - 1, PIECES) + 2)

    halos = []
    for a in range(2):
        halos.append(
            pltpu.make_async_remote_copy(
                src_ref=side.at[a, core],
                dst_ref=halo.at[a, 1],
                send_sem=hsend.at[a, 1],
                recv_sem=hrecv.at[a, 1],
                device_id=beside,
                device_id_type=MESH,
            )
        )
        halos.append(
            pltpu.make_async_remote_copy(
                src_ref=side.at[a, 1 - core],
                dst_ref=halo.at[a, 0],
                send_sem=hsend.at[a, 0],
                recv_sem=hrecv.at[a, 0],
                device_id=sibling,
                device_id_type=MESH,
            )
        )
    for copy in halos:
        copy.start()

    outs = (att_out, dq_out, dk_out, dv_out)
    srcs = (att, dq, total.at[0], total.at[1])

    def columns(h):
        return pl.ds(pl.multiple_of(h * HEAD_DIM, HEAD_DIM), HEAD_DIM)

    def slot_of(step):
        return (my_slot + step) % PIECES

    def place_of(s):
        return 2 * core + s // 8, (s // 4) % 2, s % 4

    def local(s):
        zz, cc, yy = place_of(s)
        return (zz == z) & (cc == core) & (yy == y)

    def piece(a, s):
        return srcs[a].at[pl.ds(pl.multiple_of(s * PIECE, PIECE), PIECE), :]

    def remote_copy(a, s):
        zz, cc, yy = place_of(s)
        return pltpu.make_async_remote_copy(
            src_ref=piece(a, s),
            dst_ref=outs[a].at[:, columns(head)],
            send_sem=send.at[a, s],
            recv_sem=recv.at[a, head],
            device_id={"ctx": ctx_of(x, zz, cc), "head": yy},
            device_id_type=MESH,
        )

    def send_all(a):
        def start(step, c):
            s = slot_of(step)
            mine = local(s)

            @pl.when(mine)
            def _():
                pltpu.make_async_copy(
                    piece(a, s), outs[a].at[:, columns(head)], recv.at[a, head]
                ).start()

            @pl.when(jnp.logical_not(mine))
            def _():
                remote_copy(a, s).start()

            return c

        lax.fori_loop(0, PIECES, start, 0)

    send_all(0)
    send_all(1)
    for a in range(2):
        halos[2 * a].wait_recv()
        halos[2 * a + 1].wait_recv()

        def sum_piece(s, c):
            cols = pl.ds(pl.multiple_of(s * PIECE, PIECE), PIECE)
            tot = (
                own[a, :, cols]
                + halo[a, 0, :, cols].astype(F32)
                + halo[a, 1, :, cols].astype(F32)
            )
            total[a, cols, :] = tot.T.astype(BF)
            return c

        lax.fori_loop(0, PIECES, sum_piece, 0)
        send_all(2 + a)
    for copy in halos:
        copy.wait_send()
    for a in range(4):

        def wait(h, c):
            part = outs[a].at[:, columns(h)]
            pltpu.make_async_copy(part, part, recv.at[a, h]).wait()

            @pl.when(jnp.logical_not(local(h)))
            def _():
                remote_copy(a, h).wait_send()

            return c

        lax.fori_loop(0, PIECES, wait, 0)


def scatter(att, dq, own, side):
    any_spec = pl.BlockSpec(memory_space=pl.ANY)
    out = jax.ShapeDtypeStruct((PIECE, PIECES * HEAD_DIM), BF)
    return pl.pallas_call(
        scatter_kernel,
        out_shape=(out,) * 4,
        in_specs=[pl.BlockSpec(memory_space=pltpu.VMEM)] * 4,
        out_specs=(any_spec,) * 4,
        scratch_shapes=[
            pltpu.VMEM((2, 2, HEAD_DIM, GROUP), BF),
            pltpu.VMEM((2, GROUP, HEAD_DIM), BF),
            pltpu.SemaphoreType.DMA((4, PIECES)),
            pltpu.SemaphoreType.DMA((4, PIECES)),
            pltpu.SemaphoreType.DMA((2, 2)),
            pltpu.SemaphoreType.DMA((2, 2)),
        ],
        compiler_params=pltpu.CompilerParams(
            collective_id=1, has_side_effects=True, vmem_limit_bytes=32 * 1024 * 1024
        ),
        name="to_tokens",
    )(att, dq, own, side)


def body(queries, keys_in, values, out_grad, doc_lengths):
    q, g, kw, vw = gather(queries, keys_in, values, out_grad)
    att, dq, own, side = attend(doc_lengths, q, g, kw, vw)
    return scatter(att, dq, own, side)


def solution(mesh):
    tokens = P(("ctx", "head"), None)
    return jax.shard_map(
        body,
        mesh=mesh,
        in_specs=(tokens,) * 4 + (P(),),
        out_specs=(tokens,) * 4,
        check_vma=False,
    )
```

```python
import jax
import jax.numpy as jnp
from jax import lax
from jax.experimental import pallas as pl
from jax.experimental.pallas import tpu as pltpu
from jax.sharding import PartitionSpec as P

HEAD_DIM = 128
NDOCS = 15
GROUP = 2048
PIECE = 128
PIECES = GROUP // PIECE
B = 256
TILES = GROUP // B
FOLD = TILES + 1
NEG = -1e30
SCALE = HEAD_DIM ** (-0.5)
LOG2E = 1.4426950408889634
MESH = pl.DeviceIdType.MESH
BF = jnp.bfloat16
F32 = jnp.float32


def ctx_of(x, z, core):
    return (x * 4 + z) * 2 + core


def dot_nt(a, b):
    return lax.dot_general(a, b, (((1,), (1,)), ((), ())), preferred_element_type=F32)


def dot_nn(a, b):
    return lax.dot_general(a, b, (((1,), (0,)), ((), ())), preferred_element_type=F32)


def kernel(
    lens, q_in, k_in, v_in, g_in, att_out, dq_out, dk_out, dv_out,
    q_own, g_own, k_win, v_win, scores, probs, end_row, start_row, end_lane, peaks, invs,
    att, dq, grads, far_buf, sib_buf, far_in, sib_in, total,
    send, recv, hsend, hrecv, osend, orecv, fsend, frecv, ssend, srecv,
):
    ctx = lax.axis_index("ctx")
    y = lax.axis_index("head")
    x = ctx // 8
    z = (ctx // 2) % 4
    core = ctx % 2
    half = z // 2
    my_slot = ((2 * z + core) % 4) * 4 + y
    my_head = z * 4 + y
    sibling = {"ctx": ctx_of(x, z, 1 - core), "head": y}
    far_x = jnp.where(core == 0, (x + 3) % 4, (x + 1) % 4)
    beside = {"ctx": ctx_of(far_x, z, 1 - core), "head": y}
    barrier = pltpu.get_barrier_semaphore()

    def host_of(step):
        zz = (z + step // 4) % 4
        yy = (y + step % 4) % 4
        return zz * 4 + yy, {"ctx": ctx_of(x, zz, half), "head": yy}

    def owner_of(s):
        zz, cc, yy = 2 * core + s // 8, (s // 4) % 2, s % 4
        mine = (zz == z) & (cc == core) & (yy == y)
        return mine, {"ctx": ctx_of(x, zz, cc), "head": yy}

    def greet(step, c):
        _, host = host_of(step)

        @pl.when((step > 0) | (half != core))
        def _():
            pl.semaphore_signal(barrier, inc=1, device_id=host, device_id_type=MESH)

        mine, owner = owner_of(step)

        @pl.when(jnp.logical_not(mine))
        def _():
            pl.semaphore_signal(barrier, inc=1, device_id=owner, device_id_type=MESH)

        return c

    lax.fori_loop(0, PIECES, greet, 0)
    pl.semaphore_signal(barrier, inc=1, device_id=sibling, device_id_type=MESH)
    pl.semaphore_signal(barrier, inc=1, device_id=beside, device_id_type=MESH)
    pl.semaphore_wait(barrier, 2 * jnp.where(half == core, PIECES - 1, PIECES) + 2)

    def rows_of(s, count):
        return pl.ds(pl.multiple_of(s * count, count), count)

    own = pl.ds(GROUP, GROUP)
    incoming = (k_win.at[own], q_own, v_win.at[own], g_own)
    sources = (k_in, q_in, v_in, g_in)

    def in_refs(a, step):
        head, host = host_of(step)
        return sources[a].at[:, rows_of(head, HEAD_DIM)], incoming[a].at[rows_of(my_slot, PIECE)], host

    def in_copy(a, step):
        src, dst, host = in_refs(a, step)
        return pltpu.make_async_remote_copy(
            src_ref=src, dst_ref=dst, send_sem=send.at[a, step], recv_sem=recv.at[a, my_slot],
            device_id=host, device_id_type=MESH,
        )

    for a in range(4):

        @pl.when(half == core)
        def _():
            src, dst, _ = in_refs(a, 0)
            pltpu.make_async_copy(src, dst, recv.at[a, my_slot]).start()

        @pl.when(half != core)
        def _():
            in_copy(a, 0).start()

        def start_in(step, c):
            in_copy(a, step).start()
            return c

        lax.fori_loop(1, PIECES, start_in, 0)

    bound = -((ctx // 8) * 2 + core) * GROUP
    bounds = [bound]
    for j in range(NDOCS):
        bounds.append(bounds[-1] + lens[j])

    def find_bounds(i, c):
        pos = lax.broadcasted_iota(jnp.int32, (B, 128), 0) + i * B
        first = jnp.full((B, 128), bounds[0], jnp.int32)
        last = jnp.full((B, 128), bounds[NDOCS], jnp.int32)
        lane_pos = lax.broadcasted_iota(jnp.int32, (8, B), 1) + i * B
        lane_last = jnp.full((8, B), bounds[NDOCS], jnp.int32)
        for j in range(1, NDOCS):
            first = jnp.where(pos >= bounds[j], bounds[j], first)
            k = NDOCS - j
            last = jnp.where(pos < bounds[k], bounds[k], last)
            lane_last = jnp.where(lane_pos < bounds[k], bounds[k], lane_last)
        start_row[i] = first - i * B
        end_row[i] = last - i * B
        end_lane[i] = lane_last - i * B
        return c

    lax.fori_loop(0, TILES, find_bounds, 0)

    def clear(b, c):
        grads[0, b] = jnp.zeros((HEAD_DIM, B), F32)
        grads[1, b] = jnp.zeros((HEAD_DIM, B), F32)
        return c

    lax.fori_loop(0, 3 * TILES, clear, 0)

    def wait_in(a):
        def wait(s, c):
            piece = incoming[a].at[rows_of(s, PIECE)]
            pltpu.make_async_copy(piece, piece, recv.at[a, s]).wait()
            return c

        lax.fori_loop(0, PIECES, wait, 0)

    def halo_copies(a, win):
        sib = pltpu.make_async_remote_copy(
            src_ref=win.at[own], dst_ref=win.at[rows_of(2 * core, GROUP)],
            send_sem=hsend.at[a, 0], recv_sem=hrecv.at[a, 0],
            device_id=sibling, device_id_type=MESH,
        )
        far = pltpu.make_async_remote_copy(
            src_ref=win.at[own], dst_ref=win.at[rows_of(2 * (1 - core), GROUP)],
            send_sem=hsend.at[a, 1], recv_sem=hrecv.at[a, 1],
            device_id=beside, device_id_type=MESH,
        )
        return far, sib

    lane = lax.broadcasted_iota(jnp.int32, (1, 128), 1)

    def block(win, b):
        return win[rows_of(b, B), :]

    def pair(win, i, m):
        return jnp.concatenate([block(win, i + m - 1), block(win, i + m + TILES)], axis=1)

    def split(value, right, axis):
        low = value.astype(BF)
        left = jnp.where(right, 0.0, value).astype(BF)
        return jnp.concatenate([left, low - left], axis=axis)

    def pick(both, right):
        return jnp.where(right, both[:, HEAD_DIM:], both[:, :HEAD_DIM])

    def score_tile(i, c):
        q = q_own[rows_of(i, B), :]
        q32 = q.astype(F32)
        end = end_row[i]
        first = start_row[i]
        folded = first + FOLD * B
        peak = jnp.full((B, 128), NEG, F32)
        for m in range(FOLD):
            if m == 0:
                s = dot_nt(q, block(k_win, i + TILES))
            else:
                right = end > m * B
                s = dot_nt(split(q32, right, 1), pair(k_win, i, m))
                edge = jnp.where(right, end, folded)
                left = jnp.logical_not(right)
            for h in range(2):
                col = lane + (m * B + h * 128)
                if m == 0:
                    valid = (col < end) & (col >= first)
                else:
                    valid = jnp.logical_xor(col < edge, left)
                part = jnp.where(valid, s[:, h * 128:(h + 1) * 128], NEG)
                peak = jnp.maximum(peak, part)
                scores[i, m, :, h * 128:(h + 1) * 128] = part
        peaks[i] = jnp.broadcast_to(jnp.max(peak, axis=1, keepdims=True), (B, 128))
        return c

    def output_tile(i, c):
        end = end_row[i]
        peak = peaks[i]
        acc = jnp.zeros((B, HEAD_DIM), F32)
        mass = jnp.zeros((B, 128), F32)
        for m in range(FOLD):
            parts = []
            for h in range(2):
                p = jnp.exp2((scores[i, m, :, h * 128:(h + 1) * 128] - peak) * (SCALE * LOG2E))
                mass += p
                parts.append(p.astype(BF))
            low = jnp.concatenate(parts, axis=1)
            probs[i, m] = low
            if m == 0:
                acc += dot_nn(low, block(v_win, i + TILES))
            else:
                acc += pick(dot_nn(low, pair(v_win, i, m)), end > m * B)
        inv = 1.0 / jnp.sum(mass, axis=1, keepdims=True)
        invs[i] = jnp.broadcast_to(inv, (B, 128))
        att[rows_of(i, B), :] = (acc * inv).astype(BF)
        return c

    def add_pair(a, i, m, both):
        grads[a, i + m - 1] += both[:HEAD_DIM]
        grads[a, i + m + TILES] += both[HEAD_DIM:]

    def value_tile(i, c):
        scaled = (g_own[rows_of(i, B), :].astype(F32) * invs[i]).T
        end = end_lane[i][:1]
        grads[1, i + TILES] += dot_nn(scaled.astype(BF), probs[i, 0])
        for m in range(1, FOLD):
            add_pair(1, i, m, dot_nn(split(scaled, end > m * B, 0), probs[i, m]))
        return c

    def grad_tile(i):
        rows = rows_of(i, B)
        inv = invs[i]
        g32 = g_own[rows, :].astype(F32)
        dot = jnp.sum(g32 * att[rows, :].astype(F32), axis=1, keepdims=True)
        dot = jnp.broadcast_to(dot, (B, 128))
        scaled = (q_own[rows, :].astype(F32) * (inv * SCALE)).T
        end = end_row[i]
        ends = end_lane[i][:1]
        acc = jnp.zeros((B, HEAD_DIM), F32)
        for m in range(FOLD):
            if m == 0:
                dp = dot_nt(g_own[rows, :], block(v_win, i + TILES))
            else:
                right = end > m * B
                dp = dot_nt(split(g32, right, 1), pair(v_win, i, m))
            ds = jnp.concatenate(
                [
                    (
                        probs[i, m, :, h * 128:(h + 1) * 128].astype(F32)
                        * (dp[:, h * 128:(h + 1) * 128] - dot)
                    ).astype(BF)
                    for h in range(2)
                ],
                axis=1,
            )
            if m == 0:
                acc += dot_nn(ds, block(k_win, i + TILES))
                grads[0, i + TILES] += dot_nn(scaled.astype(BF), ds)
            else:
                acc += pick(dot_nn(ds, pair(k_win, i, m)), right)
                add_pair(0, i, m, dot_nn(split(scaled, ends > m * B, 0), ds))
        dq[rows, :] = (acc * (inv * SCALE)).astype(BF)

    outs = (att_out, dq_out, dk_out, dv_out)
    ready = (att, dq, total.at[0], total.at[1])

    def out_refs(a, s):
        return ready[a].at[rows_of(s, PIECE)], outs[a].at[:, rows_of(my_head, HEAD_DIM)]

    def out_copy(a, s, owner):
        src, dst = out_refs(a, s)
        return pltpu.make_async_remote_copy(
            src_ref=src, dst_ref=dst, send_sem=osend.at[a, s], recv_sem=orecv.at[a, my_head],
            device_id=owner, device_id_type=MESH,
        )

    def start_out(a, s):
        mine, owner = owner_of(s)

        @pl.when(mine)
        def _():
            src, dst = out_refs(a, s)
            pltpu.make_async_copy(src, dst, orecv.at[a, my_head]).start()

        @pl.when(jnp.logical_not(mine))
        def _():
            out_copy(a, s, owner).start()

    def far_copy(a, t):
        return pltpu.make_async_remote_copy(
            src_ref=far_buf.at[a, t], dst_ref=far_in.at[a, t],
            send_sem=fsend.at[a, t], recv_sem=frecv.at[a, t],
            device_id=beside, device_id_type=MESH,
        )

    def send_far(a, t):
        far_buf[a, t] = grads[a, t + 2 * TILES * core].astype(BF)
        far_copy(a, t).start()

    def sib_copy(a):
        return pltpu.make_async_remote_copy(
            src_ref=sib_buf.at[a], dst_ref=sib_in.at[a],
            send_sem=ssend.at[a], recv_sem=srecv.at[a],
            device_id=sibling, device_id_type=MESH,
        )

    def send_sib(a):
        def fill(t, c):
            sib_buf[a, t] = grads[a, t + 2 * TILES * (1 - core)].astype(BF)
            return c

        lax.fori_loop(0, TILES, fill, 0)
        sib_copy(a).start()

    def finish(a):
        sib_copy(a).wait_recv()

        def add(t, c):
            far_copy(a, t).wait_recv()
            value = grads[a, t + TILES] + far_in[a, t].astype(F32) + sib_in[a, t].astype(F32)
            total[a, rows_of(t, B), :] = value.T.astype(BF)
            start_out(2 + a, 2 * t)
            start_out(2 + a, 2 * t + 1)
            return c

        lax.fori_loop(0, TILES, add, 0)

    wait_in(0)
    k_halo = halo_copies(0, k_win)
    for copy in k_halo:
        copy.start()
    wait_in(1)
    for copy in k_halo:
        copy.wait_recv()
    lax.fori_loop(0, TILES, score_tile, 0)
    wait_in(2)
    v_halo = halo_copies(1, v_win)
    for copy in v_halo:
        copy.start()
    for copy in v_halo:
        copy.wait_recv()
    lax.fori_loop(0, TILES, output_tile, 0)
    wait_in(3)

    def start_att(s, c):
        start_out(0, s)
        return c

    lax.fori_loop(0, PIECES, start_att, 0)
    lax.fori_loop(0, TILES, value_tile, 0)

    def far_values(t, c):
        send_far(1, t)
        return c

    lax.fori_loop(0, TILES, far_values, 0)
    send_sib(1)

    def grad_step(n, c):
        i = jnp.where(core == 0, n, TILES - 1 - n)
        grad_tile(i)
        start_out(1, 2 * i)
        start_out(1, 2 * i + 1)
        send_far(0, i)

        @pl.when(n == 3)
        def _():
            finish(1)

        return c

    lax.fori_loop(0, TILES, grad_step, 0)
    send_sib(0)
    finish(0)

    for copy in k_halo + v_halo:
        copy.wait_send()
    for a in range(2):
        sib_copy(a).wait_send()

        def wait_far(t, c):
            far_copy(a, t).wait_send()
            return c

        lax.fori_loop(0, TILES, wait_far, 0)
    for a in range(4):

        @pl.when(half != core)
        def _():
            in_copy(a, 0).wait_send()

        def wait_in_sent(step, c):
            in_copy(a, step).wait_send()
            return c

        lax.fori_loop(1, PIECES, wait_in_sent, 0)

        def wait_out(h, c):
            part = outs[a].at[:, rows_of(h, HEAD_DIM)]
            pltpu.make_async_copy(part, part, orecv.at[a, h]).wait()
            mine, owner = owner_of(h)

            @pl.when(jnp.logical_not(mine))
            def _():
                out_copy(a, h, owner).wait_send()

            return c

        lax.fori_loop(0, PIECES, wait_out, 0)


def body(queries, keys_in, values, out_grad, doc_lengths):
    any_spec = pl.BlockSpec(memory_space=pl.ANY)
    out = jax.ShapeDtypeStruct((PIECE, PIECES * HEAD_DIM), BF)
    own = pltpu.VMEM((GROUP, HEAD_DIM), BF)
    window = pltpu.VMEM((3 * GROUP, HEAD_DIM), BF)
    side = pltpu.VMEM((2, TILES, HEAD_DIM, B), BF)
    dma = pltpu.SemaphoreType.DMA
    return pl.pallas_call(
        kernel,
        out_shape=(out,) * 4,
        in_specs=[pl.BlockSpec(memory_space=pltpu.SMEM)] + [any_spec] * 4,
        out_specs=(any_spec,) * 4,
        scratch_shapes=[
            own, own, window, window,
            pltpu.VMEM((TILES, FOLD, B, B), F32),
            pltpu.VMEM((TILES, FOLD, B, B), BF),
            pltpu.VMEM((TILES, B, 128), jnp.int32),
            pltpu.VMEM((TILES, B, 128), jnp.int32),
            pltpu.VMEM((TILES, 8, B), jnp.int32),
            pltpu.VMEM((TILES, B, 128), F32),
            pltpu.VMEM((TILES, B, 128), F32),
            own, own,
            pltpu.VMEM((2, 3 * TILES, HEAD_DIM, B), F32),
            side, side, side, side,
            pltpu.VMEM((2, GROUP, HEAD_DIM), BF),
            dma((4, PIECES)), dma((4, PIECES)), dma((2, 2)), dma((2, 2)),
            dma((4, PIECES)), dma((4, PIECES)), dma((2, TILES)), dma((2, TILES)),
            dma((2,)), dma((2,)),
        ],
        compiler_params=pltpu.CompilerParams(
            collective_id=0, has_side_effects=True, vmem_limit_bytes=60 * 1024 * 1024
        ),
        name="attend",
    )(doc_lengths, queries, keys_in, values, out_grad)


def solution(mesh):
    tokens = P(("ctx", "head"), None)
    return jax.shard_map(
        body,
        mesh=mesh,
        in_specs=(tokens,) * 4 + (P(),),
        out_specs=(tokens,) * 4,
        check_vma=False,
    )
```

```python
import jax
import jax.numpy as jnp
from jax import lax
from jax.experimental import pallas as pl
from jax.experimental.pallas import tpu as pltpu
from jax.sharding import PartitionSpec as P

HEAD_DIM = 128
NDOCS = 15
GROUP = 2048
PIECE = 128
PIECES = GROUP // PIECE
CHUNKS = 4
CHUNK = GROUP // CHUNKS
B = 256
TILES = GROUP // B
FOLD = TILES + 1
NEG = -1e30
SCALE = HEAD_DIM ** (-0.5)
LOG2E = 1.4426950408889634
MESH = pl.DeviceIdType.MESH
BF = jnp.bfloat16
F32 = jnp.float32


def ctx_of(x, z, core):
    return (x * 4 + z) * 2 + core


def dot_nt(a, b):
    return lax.dot_general(a, b, (((1,), (1,)), ((), ())), preferred_element_type=F32)


def dot_nn(a, b):
    return lax.dot_general(a, b, (((1,), (0,)), ((), ())), preferred_element_type=F32)


def kernel(
    lens, q_in, k_in, v_in, g_in, att_out, dq_out, dk_out, dv_out,
    q_own, g_own, k_win, v_win, scores, probs, end_row, start_row, end_lane, peaks, invs,
    att, dq, grads, far_buf, sib_buf, far_in, sib_in, total,
    send, recv, hsend, hrecv, osend, orecv, fsend, frecv, ssend, srecv,
):
    ctx = lax.axis_index("ctx")
    y = lax.axis_index("head")
    x = ctx // 8
    z = (ctx // 2) % 4
    core = ctx % 2
    half = z // 2
    my_slot = ((2 * z + core) % 4) * 4 + y
    my_head = z * 4 + y
    sibling = {"ctx": ctx_of(x, z, 1 - core), "head": y}
    far_x = jnp.where(core == 0, (x + 3) % 4, (x + 1) % 4)
    beside = {"ctx": ctx_of(far_x, z, 1 - core), "head": y}
    barrier = pltpu.get_barrier_semaphore()

    def host_of(step):
        zz = (z + step // 4) % 4
        yy = (y + step % 4) % 4
        return zz * 4 + yy, {"ctx": ctx_of(x, zz, half), "head": yy}

    def owner_of(s):
        zz, cc, yy = 2 * core + s // 8, (s // 4) % 2, s % 4
        mine = (zz == z) & (cc == core) & (yy == y)
        return mine, {"ctx": ctx_of(x, zz, cc), "head": yy}

    def greet(step, c):
        mine, owner = owner_of(step)

        @pl.when(jnp.logical_not(mine))
        def _():
            pl.semaphore_signal(barrier, inc=1, device_id=owner, device_id_type=MESH)

        return c

    lax.fori_loop(0, PIECES, greet, 0)
    pl.semaphore_signal(barrier, inc=1, device_id=sibling, device_id_type=MESH)
    pl.semaphore_signal(barrier, inc=1, device_id=beside, device_id_type=MESH)
    pl.semaphore_wait(barrier, jnp.where(half == core, PIECES - 1, PIECES) + 2)

    def rows_of(s, count):
        return pl.ds(pl.multiple_of(s * count, count), count)

    own = pl.ds(GROUP, GROUP)
    incoming = (k_win.at[own], q_own, v_win.at[own], g_own)
    sources = (k_in, q_in, v_in, g_in)

    def in_refs(a, step):
        head, host = host_of(step)
        return sources[a].at[:, rows_of(head, HEAD_DIM)], incoming[a].at[rows_of(my_slot, PIECE)], host

    def in_copy(a, step):
        src, dst, host = in_refs(a, step)
        return pltpu.make_async_remote_copy(
            src_ref=src, dst_ref=dst, send_sem=send.at[a, step], recv_sem=recv.at[a, my_slot],
            device_id=host, device_id_type=MESH,
        )

    def start_in_all(a):
        @pl.when(half == core)
        def _():
            src, dst, _ = in_refs(a, 0)
            pltpu.make_async_copy(src, dst, recv.at[a, my_slot]).start()

        @pl.when(half != core)
        def _():
            in_copy(a, 0).start()

        def start_in(step, c):
            in_copy(a, step).start()
            return c

        lax.fori_loop(1, PIECES, start_in, 0)

    for a in (0, 2, 1, 3):
        start_in_all(a)

    bound = -((ctx // 8) * 2 + core) * GROUP
    bounds = [bound]
    for j in range(NDOCS):
        bounds.append(bounds[-1] + lens[j])

    def find_bounds(i, c):
        pos = lax.broadcasted_iota(jnp.int32, (B, 128), 0) + i * B
        first = jnp.full((B, 128), bounds[0], jnp.int32)
        last = jnp.full((B, 128), bounds[NDOCS], jnp.int32)
        lane_pos = lax.broadcasted_iota(jnp.int32, (8, B), 1) + i * B
        lane_last = jnp.full((8, B), bounds[NDOCS], jnp.int32)
        for j in range(1, NDOCS):
            first = jnp.where(pos >= bounds[j], bounds[j], first)
            k = NDOCS - j
            last = jnp.where(pos < bounds[k], bounds[k], last)
            lane_last = jnp.where(lane_pos < bounds[k], bounds[k], lane_last)
        start_row[i] = first - i * B
        end_row[i] = last - i * B
        end_lane[i] = lane_last - i * B
        return c

    lax.fori_loop(0, TILES, find_bounds, 0)

    def clear(b, c):
        grads[0, b] = jnp.zeros((HEAD_DIM, B), F32)
        grads[1, b] = jnp.zeros((HEAD_DIM, B), F32)
        return c

    lax.fori_loop(0, 3 * TILES, clear, 0)

    def wait_piece(a, s):
        piece = incoming[a].at[rows_of(s, PIECE)]
        pltpu.make_async_copy(piece, piece, recv.at[a, s]).wait()

    def wait_in(a):
        def wait(s, c):
            wait_piece(a, s)
            return c

        lax.fori_loop(0, PIECES, wait, 0)

    order = jnp.where((z - 2 * core) % 4 == 0, 0, 2)

    def halo_copies(a, n):
        win = (k_win, v_win)[a]
        chunk = (order + n) % CHUNKS
        src = win.at[rows_of(CHUNKS + chunk, CHUNK)]
        sib = pltpu.make_async_remote_copy(
            src_ref=src, dst_ref=win.at[rows_of(2 * core * CHUNKS + chunk, CHUNK)],
            send_sem=hsend.at[a, 0, chunk], recv_sem=hrecv.at[a, 0, chunk],
            device_id=sibling, device_id_type=MESH,
        )
        far = pltpu.make_async_remote_copy(
            src_ref=src, dst_ref=win.at[rows_of(2 * (1 - core) * CHUNKS + chunk, CHUNK)],
            send_sem=hsend.at[a, 1, chunk], recv_sem=hrecv.at[a, 1, chunk],
            device_id=beside, device_id_type=MESH,
        )
        return far, sib

    def pass_on(a, n):
        def wait(s, c):
            wait_piece(2 * a, (order + n) % CHUNKS * CHUNKS + s)
            return c

        lax.fori_loop(0, CHUNKS, wait, 0)
        for copy in halo_copies(a, n):
            copy.start()

    def wait_halo(a):
        def wait(n, c):
            for copy in halo_copies(a, n):
                copy.wait_recv()
            return c

        lax.fori_loop(0, CHUNKS, wait, 0)

    lane = lax.broadcasted_iota(jnp.int32, (1, 128), 1)

    def block(win, b):
        return win[rows_of(b, B), :]

    def pair(win, i, m):
        return jnp.concatenate([block(win, i + m - 1), block(win, i + m + TILES)], axis=1)

    def split(value, right, axis):
        low = value.astype(BF)
        left = jnp.where(right, 0.0, value).astype(BF)
        return jnp.concatenate([left, low - left], axis=axis)

    def pick(both, right):
        return jnp.where(right, both[:, HEAD_DIM:], both[:, :HEAD_DIM])

    def score_tile(i):
        q = q_own[rows_of(i, B), :]
        q32 = q.astype(F32)
        end = end_row[i]
        first = start_row[i]
        folded = first + FOLD * B
        peak = jnp.full((B, 128), NEG, F32)
        for m in range(FOLD):
            if m == 0:
                s = dot_nt(q, block(k_win, i + TILES))
            else:
                right = end > m * B
                s = dot_nt(split(q32, right, 1), pair(k_win, i, m))
                sign = jnp.where(right, 1.0, -1.0)
                edge = jnp.where(right, -end, folded - 1).astype(F32)
            for h in range(2):
                col = lane + (m * B + h * 128)
                if m == 0:
                    valid = (col < end) & (col >= first)
                else:
                    valid = (col.astype(F32) * sign + edge) < 0.0
                part = jnp.where(valid, s[:, h * 128:(h + 1) * 128], NEG)
                peak = jnp.maximum(peak, part)
                scores[i, m, :, h * 128:(h + 1) * 128] = part
        peaks[i] = jnp.broadcast_to(jnp.max(peak, axis=1, keepdims=True), (B, 128))

    def output_tile(i):
        end = end_row[i]
        peak = peaks[i]
        acc = jnp.zeros((B, HEAD_DIM), F32)
        mass = jnp.zeros((B, 128), F32)
        for m in range(FOLD):
            parts = []
            for h in range(2):
                p = jnp.exp2((scores[i, m, :, h * 128:(h + 1) * 128] - peak) * (SCALE * LOG2E))
                mass += p
                parts.append(p.astype(BF))
            low = jnp.concatenate(parts, axis=1)
            probs[i, m] = low
            if m == 0:
                acc += dot_nn(low, block(v_win, i + TILES))
            else:
                acc += pick(dot_nn(low, pair(v_win, i, m)), end > m * B)
        inv = 1.0 / jnp.sum(mass, axis=1, keepdims=True)
        invs[i] = jnp.broadcast_to(inv, (B, 128))
        att[rows_of(i, B), :] = (acc * inv).astype(BF)

    def add_pair(a, i, m, both):
        grads[a, i + m - 1] += both[:HEAD_DIM]
        grads[a, i + m + TILES] += both[HEAD_DIM:]

    def value_tile(i):
        scaled = (g_own[rows_of(i, B), :].astype(F32) * invs[i]).T
        end = end_lane[i][:1]
        grads[1, i + TILES] += dot_nn(scaled.astype(BF), probs[i, 0])
        for m in range(1, FOLD):
            add_pair(1, i, m, dot_nn(split(scaled, end > m * B, 0), probs[i, m]))

    def grad_tile(i):
        rows = rows_of(i, B)
        inv = invs[i]
        g32 = g_own[rows, :].astype(F32)
        dot = jnp.sum(g32 * att[rows, :].astype(F32), axis=1, keepdims=True)
        dot = jnp.broadcast_to(dot, (B, 128))
        scaled = (q_own[rows, :].astype(F32) * (inv * SCALE)).T
        end = end_row[i]
        ends = end_lane[i][:1]
        acc = jnp.zeros((B, HEAD_DIM), F32)
        for m in range(FOLD):
            if m == 0:
                dp = dot_nt(g_own[rows, :], block(v_win, i + TILES))
            else:
                dp = dot_nt(split(g32, end > m * B, 1), pair(v_win, i, m))
            for h in range(2):
                half_cols = slice(h * 128, (h + 1) * 128)
                probs[i, m, :, half_cols] = (
                    probs[i, m, :, half_cols].astype(F32) * (dp[:, half_cols] - dot)
                ).astype(BF)
        acc = dot_nn(probs[i, 0], block(k_win, i + TILES))
        for m in range(1, FOLD):
            acc += pick(dot_nn(probs[i, m], pair(k_win, i, m)), end > m * B)
        grads[0, i + TILES] += dot_nn(scaled.astype(BF), probs[i, 0])
        for m in range(1, FOLD):
            add_pair(0, i, m, dot_nn(split(scaled, ends > m * B, 0), probs[i, m]))
        dq[rows, :] = (acc * (inv * SCALE)).astype(BF)

    outs = (att_out, dq_out, dk_out, dv_out)
    ready = (att, dq, total.at[0], total.at[1])

    def out_refs(a, s):
        return ready[a].at[rows_of(s, PIECE)], outs[a].at[:, rows_of(my_head, HEAD_DIM)]

    def out_copy(a, s, owner):
        src, dst = out_refs(a, s)
        return pltpu.make_async_remote_copy(
            src_ref=src, dst_ref=dst, send_sem=osend.at[a, s], recv_sem=orecv.at[a, my_head],
            device_id=owner, device_id_type=MESH,
        )

    def start_out(a, s):
        mine, owner = owner_of(s)

        @pl.when(mine)
        def _():
            src, dst = out_refs(a, s)
            pltpu.make_async_copy(src, dst, orecv.at[a, my_head]).start()

        @pl.when(jnp.logical_not(mine))
        def _():
            out_copy(a, s, owner).start()

    def far_copy(a, t):
        return pltpu.make_async_remote_copy(
            src_ref=far_buf.at[a, t], dst_ref=far_in.at[a, t],
            send_sem=fsend.at[a, t], recv_sem=frecv.at[a, t],
            device_id=beside, device_id_type=MESH,
        )

    def send_far(a, t):
        far_buf[a, t] = grads[a, t + 2 * TILES * core].astype(BF)
        far_copy(a, t).start()

    def sib_copy(a, t):
        return pltpu.make_async_remote_copy(
            src_ref=sib_buf.at[a, t], dst_ref=sib_in.at[a, t],
            send_sem=ssend.at[a, t], recv_sem=srecv.at[a, t],
            device_id=sibling, device_id_type=MESH,
        )

    def send_sib(a):
        def fill(t, c):
            sib_buf[a, t] = grads[a, t + 2 * TILES * (1 - core)].astype(BF)
            sib_copy(a, t).start()
            return c

        lax.fori_loop(0, TILES, fill, 0)

    def finish(a):
        def add(t, c):
            far_copy(a, t).wait_recv()
            sib_copy(a, t).wait_recv()
            value = grads[a, t + TILES] + far_in[a, t].astype(F32) + sib_in[a, t].astype(F32)
            total[a, rows_of(t, B), :] = value.T.astype(BF)
            start_out(2 + a, 2 * t)
            start_out(2 + a, 2 * t + 1)
            return c

        lax.fori_loop(0, TILES, add, 0)

    def ordered(n):
        return jnp.where(core == 0, n, TILES - 1 - n)

    def key_step(n, c):
        pass_on(0, n)
        return c

    lax.fori_loop(0, CHUNKS, key_step, 0)

    def val_step(n, c):
        pass_on(1, n)
        return c

    lax.fori_loop(0, CHUNKS, val_step, 0)
    wait_in(1)
    wait_halo(0)

    def score_step(i, c):
        score_tile(i)

        return c

    lax.fori_loop(0, TILES, score_step, 0)
    wait_halo(1)

    def output_step(i, c):
        output_tile(i)
        start_out(0, 2 * i)
        start_out(0, 2 * i + 1)
        return c

    lax.fori_loop(0, TILES, output_step, 0)
    wait_in(3)

    def value_step(n, c):
        i = ordered(n)
        value_tile(i)
        send_far(1, i)
        return c

    lax.fori_loop(0, TILES, value_step, 0)
    send_sib(1)

    def grad_step(n, c):
        i = ordered(n)
        grad_tile(i)
        start_out(1, 2 * i)
        start_out(1, 2 * i + 1)
        send_far(0, i)

        @pl.when(n == 2)
        def _():
            finish(1)

        return c

    lax.fori_loop(0, TILES, grad_step, 0)
    send_sib(0)
    finish(0)

    for a in range(2):

        def wait_halo_sent(n, c):
            for copy in halo_copies(a, n):
                copy.wait_send()
            return c

        lax.fori_loop(0, CHUNKS, wait_halo_sent, 0)

        def wait_sides(t, c):
            far_copy(a, t).wait_send()
            sib_copy(a, t).wait_send()
            return c

        lax.fori_loop(0, TILES, wait_sides, 0)
    for a in range(4):

        @pl.when(half != core)
        def _():
            in_copy(a, 0).wait_send()

        def wait_in_sent(step, c):
            in_copy(a, step).wait_send()
            return c

        lax.fori_loop(1, PIECES, wait_in_sent, 0)

        def wait_out(h, c):
            part = outs[a].at[:, rows_of(h, HEAD_DIM)]
            pltpu.make_async_copy(part, part, orecv.at[a, h]).wait()
            mine, owner = owner_of(h)

            @pl.when(jnp.logical_not(mine))
            def _():
                out_copy(a, h, owner).wait_send()

            return c

        lax.fori_loop(0, PIECES, wait_out, 0)


def place(*refs):
    for a in range(4):
        refs[4 + a][...] = refs[a][...]


def body(queries, keys_in, values, out_grad, doc_lengths):
    any_spec = pl.BlockSpec(memory_space=pl.ANY)
    out = jax.ShapeDtypeStruct((PIECE, PIECES * HEAD_DIM), BF)
    own = pltpu.VMEM((GROUP, HEAD_DIM), BF)
    window = pltpu.VMEM((3 * GROUP, HEAD_DIM), BF)
    side = pltpu.VMEM((2, TILES, HEAD_DIM, B), BF)
    dma = pltpu.SemaphoreType.DMA
    results = pl.pallas_call(
        kernel,
        out_shape=(out,) * 4,
        in_specs=[pl.BlockSpec(memory_space=pltpu.SMEM)] + [any_spec] * 4,
        out_specs=(any_spec,) * 4,
        scratch_shapes=[
            own, own, window, window,
            pltpu.VMEM((TILES, FOLD, B, B), F32),
            pltpu.VMEM((TILES, FOLD, B, B), BF),
            pltpu.VMEM((TILES, B, 128), jnp.int32),
            pltpu.VMEM((TILES, B, 128), jnp.int32),
            pltpu.VMEM((TILES, 8, B), jnp.int32),
            pltpu.VMEM((TILES, B, 128), F32),
            pltpu.VMEM((TILES, B, 128), F32),
            own, own,
            pltpu.VMEM((2, 3 * TILES, HEAD_DIM, B), F32),
            side, side, side, side,
            pltpu.VMEM((2, GROUP, HEAD_DIM), BF),
            dma((4, PIECES)), dma((4, PIECES)), dma((2, 2, CHUNKS)), dma((2, 2, CHUNKS)),
            dma((4, PIECES)), dma((4, PIECES)), dma((2, TILES)), dma((2, TILES)),
            dma((2, TILES)), dma((2, TILES)),
        ],
        compiler_params=pltpu.CompilerParams(
            collective_id=0, has_side_effects=True, vmem_limit_bytes=60 * 1024 * 1024
        ),
        name="attend",
    )(doc_lengths, queries, keys_in, values, out_grad)
    rows = pl.BlockSpec((PIECE // 2, PIECES * HEAD_DIM), lambda i: (i, 0))
    return pl.pallas_call(
        place, grid=(2,), out_shape=(out,) * 4, in_specs=[rows] * 4, out_specs=(rows,) * 4, name="place"
    )(*results)


def solution(mesh):
    tokens = P(("ctx", "head"), None)
    return jax.shard_map(
        body,
        mesh=mesh,
        in_specs=(tokens,) * 4 + (P(),),
        out_specs=(tokens,) * 4,
        check_vma=False,
    )
```

```python
import jax
import jax.numpy as jnp
from jax import lax
from jax.experimental import pallas as pl
from jax.experimental.pallas import tpu as pltpu
from jax.sharding import PartitionSpec as P

HEAD_DIM = 128
NDOCS = 15
GROUP = 2048
PIECE = 128
PIECES = GROUP // PIECE
CHUNKS = 4
CHUNK = GROUP // CHUNKS
B = 256
TILES = GROUP // B
FOLD = TILES + 1
NEG = -1e30
SCALE = HEAD_DIM ** (-0.5)
LOG2E = 1.4426950408889634
MESH = pl.DeviceIdType.MESH
BF = jnp.bfloat16
F32 = jnp.float32


def ctx_of(x, z, core):
    return (x * 4 + z) * 2 + core


def dot_nt(a, b):
    return lax.dot_general(a, b, (((1,), (1,)), ((), ())), preferred_element_type=F32)


def dot_nn(a, b):
    return lax.dot_general(a, b, (((1,), (0,)), ((), ())), preferred_element_type=F32)


def kernel(
    lens, q_in, k_in, v_in, g_in, att_out, dq_out, dk_out, dv_out,
    q_own, g_own, k_win, v_win, scores, probs, end_row, start_row, end_lane, peaks, invs,
    att, dq, grads, far_buf, sib_buf, far_in, sib_in, total,
    send, recv, hsend, hrecv, osend, orecv, fsend, frecv, ssend, srecv,
):
    ctx = lax.axis_index("ctx")
    y = lax.axis_index("head")
    x = ctx // 8
    z = (ctx // 2) % 4
    core = ctx % 2
    half = z // 2
    my_slot = ((2 * z + core) % 4) * 4 + y
    my_head = z * 4 + y
    sibling = {"ctx": ctx_of(x, z, 1 - core), "head": y}
    far_x = jnp.where(core == 0, (x + 3) % 4, (x + 1) % 4)
    beside = {"ctx": ctx_of(far_x, z, 1 - core), "head": y}
    barrier = pltpu.get_barrier_semaphore()

    def host_of(step):
        zz = (z + step // 4) % 4
        yy = (y + step % 4) % 4
        return zz * 4 + yy, {"ctx": ctx_of(x, zz, half), "head": yy}

    def owner_of(s):
        zz, cc, yy = 2 * core + s // 8, (s // 4) % 2, s % 4
        mine = (zz == z) & (cc == core) & (yy == y)
        return mine, {"ctx": ctx_of(x, zz, cc), "head": yy}

    def greet(step, c):
        mine, owner = owner_of(step)

        @pl.when(jnp.logical_not(mine))
        def _():
            pl.semaphore_signal(barrier, inc=1, device_id=owner, device_id_type=MESH)

        return c

    lax.fori_loop(0, PIECES, greet, 0)
    pl.semaphore_signal(barrier, inc=1, device_id=sibling, device_id_type=MESH)
    pl.semaphore_signal(barrier, inc=1, device_id=beside, device_id_type=MESH)
    pl.semaphore_wait(barrier, jnp.where(half == core, PIECES - 1, PIECES) + 2)

    def rows_of(s, count):
        return pl.ds(pl.multiple_of(s * count, count), count)

    own = pl.ds(GROUP, GROUP)
    incoming = (k_win.at[own], q_own, v_win.at[own], g_own)
    sources = (k_in, q_in, v_in, g_in)

    def in_refs(a, step):
        head, host = host_of(step)
        return sources[a].at[:, rows_of(head, HEAD_DIM)], incoming[a].at[rows_of(my_slot, PIECE)], host

    def in_copy(a, step):
        src, dst, host = in_refs(a, step)
        return pltpu.make_async_remote_copy(
            src_ref=src, dst_ref=dst, send_sem=send.at[a, step], recv_sem=recv.at[a, my_slot],
            device_id=host, device_id_type=MESH,
        )

    def start_in_all(a):
        @pl.when(half == core)
        def _():
            src, dst, _ = in_refs(a, 0)
            pltpu.make_async_copy(src, dst, recv.at[a, my_slot]).start()

        @pl.when(half != core)
        def _():
            in_copy(a, 0).start()

        def start_in(step, c):
            in_copy(a, step).start()
            return c

        lax.fori_loop(1, PIECES, start_in, 0)

    for a in (0, 2, 1, 3):
        start_in_all(a)

    bound = -((ctx // 8) * 2 + core) * GROUP
    bounds = [bound]
    for j in range(NDOCS):
        bounds.append(bounds[-1] + lens[j])

    def find_bounds(i, c):
        pos = lax.broadcasted_iota(jnp.int32, (B, 128), 0) + i * B
        first = jnp.full((B, 128), bounds[0], jnp.int32)
        last = jnp.full((B, 128), bounds[NDOCS], jnp.int32)
        lane_pos = lax.broadcasted_iota(jnp.int32, (8, B), 1) + i * B
        lane_last = jnp.full((8, B), bounds[NDOCS], jnp.int32)
        for j in range(1, NDOCS):
            first = jnp.where(pos >= bounds[j], bounds[j], first)
            k = NDOCS - j
            last = jnp.where(pos < bounds[k], bounds[k], last)
            lane_last = jnp.where(lane_pos < bounds[k], bounds[k], lane_last)
        start_row[i] = first - i * B
        end_row[i] = last - i * B
        end_lane[i] = lane_last - i * B
        return c

    lax.fori_loop(0, TILES, find_bounds, 0)

    def clear(b, c):
        grads[0, b] = jnp.zeros((HEAD_DIM, B), F32)
        grads[1, b] = jnp.zeros((HEAD_DIM, B), F32)
        return c

    lax.fori_loop(0, 3 * TILES, clear, 0)

    def wait_piece(a, s):
        piece = incoming[a].at[rows_of(s, PIECE)]
        pltpu.make_async_copy(piece, piece, recv.at[a, s]).wait()

    def wait_in(a):
        def wait(s, c):
            wait_piece(a, s)
            return c

        lax.fori_loop(0, PIECES, wait, 0)

    order = jnp.where((z - 2 * core) % 4 == 0, 0, 2)

    def halo_copies(a, n):
        win = (k_win, v_win)[a]
        chunk = (order + n) % CHUNKS
        src = win.at[rows_of(CHUNKS + chunk, CHUNK)]
        sib = pltpu.make_async_remote_copy(
            src_ref=src, dst_ref=win.at[rows_of(2 * core * CHUNKS + chunk, CHUNK)],
            send_sem=hsend.at[a, 0, chunk], recv_sem=hrecv.at[a, 0, chunk],
            device_id=sibling, device_id_type=MESH,
        )
        far = pltpu.make_async_remote_copy(
            src_ref=src, dst_ref=win.at[rows_of(2 * (1 - core) * CHUNKS + chunk, CHUNK)],
            send_sem=hsend.at[a, 1, chunk], recv_sem=hrecv.at[a, 1, chunk],
            device_id=beside, device_id_type=MESH,
        )
        return far, sib

    def pass_on(a, n):
        def wait(s, c):
            wait_piece(2 * a, (order + n) % CHUNKS * CHUNKS + s)
            return c

        lax.fori_loop(0, CHUNKS, wait, 0)
        for copy in halo_copies(a, n):
            copy.start()

    def wait_halo(a):
        def wait(n, c):
            for copy in halo_copies(a, n):
                copy.wait_recv()
            return c

        lax.fori_loop(0, CHUNKS, wait, 0)

    lane = lax.broadcasted_iota(jnp.int32, (1, 128), 1)

    def block(win, b):
        return win[rows_of(b, B), :]

    def pair(win, i, m):
        return jnp.concatenate([block(win, i + m - 1), block(win, i + m + TILES)], axis=1)

    def split(value, right, axis):
        low = value.astype(BF)
        left = jnp.where(right, 0.0, value).astype(BF)
        return jnp.concatenate([left, low - left], axis=axis)

    def pick(both, right):
        return jnp.where(right, both[:, HEAD_DIM:], both[:, :HEAD_DIM])

    def score_tile(i):
        q = q_own[rows_of(i, B), :]
        q32 = q.astype(F32)
        end = end_row[i]
        first = start_row[i]
        folded = first + FOLD * B
        peak = jnp.full((B, 128), NEG, F32)
        for m in range(FOLD):
            if m == 0:
                s = dot_nt(q, block(k_win, i + TILES))
            else:
                right = end > m * B
                s = dot_nt(split(q32, right, 1), pair(k_win, i, m))
                sign = jnp.where(right, 1.0, -1.0)
                edge = jnp.where(right, -end, folded - 1).astype(F32)
            for h in range(2):
                col = lane + (m * B + h * 128)
                if m == 0:
                    valid = (col < end) & (col >= first)
                else:
                    valid = (col.astype(F32) * sign + edge) < 0.0
                part = jnp.where(valid, s[:, h * 128:(h + 1) * 128], NEG)
                peak = jnp.maximum(peak, part)
                scores[i, m, :, h * 128:(h + 1) * 128] = part
        peaks[i] = jnp.broadcast_to(jnp.max(peak, axis=1, keepdims=True), (B, 128))

    def output_tile(i):
        end = end_row[i]
        peak = peaks[i]
        acc = jnp.zeros((B, HEAD_DIM), F32)
        mass = jnp.zeros((B, 128), F32)
        for m in range(FOLD):
            parts = []
            for h in range(2):
                p = jnp.exp2((scores[i, m, :, h * 128:(h + 1) * 128] - peak) * (SCALE * LOG2E))
                mass += p
                parts.append(p.astype(BF))
            low = jnp.concatenate(parts, axis=1)
            probs[i, m] = low
            if m == 0:
                acc += dot_nn(low, block(v_win, i + TILES))
            else:
                acc += pick(dot_nn(low, pair(v_win, i, m)), end > m * B)
        inv = 1.0 / jnp.sum(mass, axis=1, keepdims=True)
        invs[i] = jnp.broadcast_to(inv, (B, 128))
        att[rows_of(i, B), :] = (acc * inv).astype(BF)

    def add_pair(a, i, m, both):
        grads[a, i + m - 1] += both[:HEAD_DIM]
        grads[a, i + m + TILES] += both[HEAD_DIM:]

    def value_tile(i):
        scaled = (g_own[rows_of(i, B), :].astype(F32) * invs[i]).T
        end = end_lane[i][:1]
        grads[1, i + TILES] += dot_nn(scaled.astype(BF), probs[i, 0])
        for m in range(1, FOLD):
            add_pair(1, i, m, dot_nn(split(scaled, end > m * B, 0), probs[i, m]))

    def grad_tile(i):
        rows = rows_of(i, B)
        inv = invs[i]
        g32 = g_own[rows, :].astype(F32)
        dot = jnp.sum(g32 * att[rows, :].astype(F32), axis=1, keepdims=True)
        dot = jnp.broadcast_to(dot, (B, 128))
        scaled = (q_own[rows, :].astype(F32) * (inv * SCALE)).T
        end = end_row[i]
        ends = end_lane[i][:1]
        acc = jnp.zeros((B, HEAD_DIM), F32)
        for m in range(FOLD):
            if m == 0:
                dp = dot_nt(g_own[rows, :], block(v_win, i + TILES))
            else:
                dp = dot_nt(split(g32, end > m * B, 1), pair(v_win, i, m))
            for h in range(2):
                half_cols = slice(h * 128, (h + 1) * 128)
                probs[i, m, :, half_cols] *= (dp[:, half_cols] - dot).astype(BF)
        acc = dot_nn(probs[i, 0], block(k_win, i + TILES))
        for m in range(1, FOLD):
            acc += pick(dot_nn(probs[i, m], pair(k_win, i, m)), end > m * B)
        grads[0, i + TILES] += dot_nn(scaled.astype(BF), probs[i, 0])
        for m in range(1, FOLD):
            add_pair(0, i, m, dot_nn(split(scaled, ends > m * B, 0), probs[i, m]))
        dq[rows, :] = (acc * (inv * SCALE)).astype(BF)

    outs = (att_out, dq_out, dk_out, dv_out)
    ready = (att, dq, total.at[0], total.at[1])

    def out_refs(a, s):
        return ready[a].at[rows_of(s, PIECE)], outs[a].at[:, rows_of(my_head, HEAD_DIM)]

    def out_copy(a, s, owner):
        src, dst = out_refs(a, s)
        return pltpu.make_async_remote_copy(
            src_ref=src, dst_ref=dst, send_sem=osend.at[a, s], recv_sem=orecv.at[a, my_head],
            device_id=owner, device_id_type=MESH,
        )

    def start_out(a, s):
        mine, owner = owner_of(s)

        @pl.when(mine)
        def _():
            src, dst = out_refs(a, s)
            pltpu.make_async_copy(src, dst, orecv.at[a, my_head]).start()

        @pl.when(jnp.logical_not(mine))
        def _():
            out_copy(a, s, owner).start()

    def far_copy(a, t):
        return pltpu.make_async_remote_copy(
            src_ref=far_buf.at[a, t], dst_ref=far_in.at[a, t],
            send_sem=fsend.at[a, t], recv_sem=frecv.at[a, t],
            device_id=beside, device_id_type=MESH,
        )

    def send_far(a, t):
        far_buf[a, t] = grads[a, t + 2 * TILES * core].astype(BF)
        far_copy(a, t).start()

    def sib_copy(a, t):
        return pltpu.make_async_remote_copy(
            src_ref=sib_buf.at[a, t], dst_ref=sib_in.at[a, t],
            send_sem=ssend.at[a, t], recv_sem=srecv.at[a, t],
            device_id=sibling, device_id_type=MESH,
        )

    def send_sib(a):
        def fill(t, c):
            sib_buf[a, t] = grads[a, t + 2 * TILES * (1 - core)].astype(BF)
            sib_copy(a, t).start()
            return c

        lax.fori_loop(0, TILES, fill, 0)

    def finish(a):
        def add(t, c):
            far_copy(a, t).wait_recv()
            sib_copy(a, t).wait_recv()
            value = grads[a, t + TILES] + far_in[a, t].astype(F32) + sib_in[a, t].astype(F32)
            total[a, rows_of(t, B), :] = value.T.astype(BF)
            start_out(2 + a, 2 * t)
            start_out(2 + a, 2 * t + 1)
            return c

        lax.fori_loop(0, TILES, add, 0)

    def ordered(n):
        return jnp.where(core == 0, n, TILES - 1 - n)

    def key_step(n, c):
        pass_on(0, n)
        return c

    lax.fori_loop(0, CHUNKS, key_step, 0)

    def val_step(n, c):
        pass_on(1, n)
        return c

    lax.fori_loop(0, CHUNKS, val_step, 0)
    wait_in(1)
    wait_halo(0)

    def score_step(i, c):
        score_tile(i)

        return c

    lax.fori_loop(0, TILES, score_step, 0, unroll=2)
    wait_halo(1)

    def output_step(i, c):
        output_tile(i)
        start_out(0, 2 * i)
        start_out(0, 2 * i + 1)
        return c

    lax.fori_loop(0, TILES, output_step, 0)
    wait_in(3)

    def value_step(n, c):
        i = ordered(n)
        value_tile(i)
        send_far(1, i)
        return c

    lax.fori_loop(0, TILES, value_step, 0)
    send_sib(1)

    def grad_step(n, c):
        i = ordered(n)
        grad_tile(i)
        start_out(1, 2 * i)
        start_out(1, 2 * i + 1)
        send_far(0, i)

        @pl.when(n == 2)
        def _():
            finish(1)

        return c

    lax.fori_loop(0, TILES, grad_step, 0)
    send_sib(0)
    finish(0)

    for a in range(2):

        def wait_halo_sent(n, c):
            for copy in halo_copies(a, n):
                copy.wait_send()
            return c

        lax.fori_loop(0, CHUNKS, wait_halo_sent, 0)

        def wait_sides(t, c):
            far_copy(a, t).wait_send()
            sib_copy(a, t).wait_send()
            return c

        lax.fori_loop(0, TILES, wait_sides, 0)
    for a in range(4):

        @pl.when(half != core)
        def _():
            in_copy(a, 0).wait_send()

        def wait_in_sent(step, c):
            in_copy(a, step).wait_send()
            return c

        lax.fori_loop(1, PIECES, wait_in_sent, 0)

        def wait_out(h, c):
            part = outs[a].at[:, rows_of(h, HEAD_DIM)]
            pltpu.make_async_copy(part, part, orecv.at[a, h]).wait()
            mine, owner = owner_of(h)

            @pl.when(jnp.logical_not(mine))
            def _():
                out_copy(a, h, owner).wait_send()

            return c

        lax.fori_loop(0, PIECES, wait_out, 0)


def place(*refs):
    for a in range(4):
        refs[4 + a][...] = refs[a][...]


def body(queries, keys_in, values, out_grad, doc_lengths):
    any_spec = pl.BlockSpec(memory_space=pl.ANY)
    out = jax.ShapeDtypeStruct((PIECE, PIECES * HEAD_DIM), BF)
    own = pltpu.VMEM((GROUP, HEAD_DIM), BF)
    window = pltpu.VMEM((3 * GROUP, HEAD_DIM), BF)
    side = pltpu.VMEM((2, TILES, HEAD_DIM, B), BF)
    dma = pltpu.SemaphoreType.DMA
    results = pl.pallas_call(
        kernel,
        out_shape=(out,) * 4,
        in_specs=[pl.BlockSpec(memory_space=pltpu.SMEM)] + [any_spec] * 4,
        out_specs=(any_spec,) * 4,
        scratch_shapes=[
            own, own, window, window,
            pltpu.VMEM((TILES, FOLD, B, B), F32),
            pltpu.VMEM((TILES, FOLD, B, B), BF),
            pltpu.VMEM((TILES, B, 128), jnp.int32),
            pltpu.VMEM((TILES, B, 128), jnp.int32),
            pltpu.VMEM((TILES, 8, B), jnp.int32),
            pltpu.VMEM((TILES, B, 128), F32),
            pltpu.VMEM((TILES, B, 128), F32),
            own, own,
            pltpu.VMEM((2, 3 * TILES, HEAD_DIM, B), F32),
            side, side, side, side,
            pltpu.VMEM((2, GROUP, HEAD_DIM), BF),
            dma((4, PIECES)), dma((4, PIECES)), dma((2, 2, CHUNKS)), dma((2, 2, CHUNKS)),
            dma((4, PIECES)), dma((4, PIECES)), dma((2, TILES)), dma((2, TILES)),
            dma((2, TILES)), dma((2, TILES)),
        ],
        compiler_params=pltpu.CompilerParams(
            collective_id=0, has_side_effects=True, vmem_limit_bytes=60 * 1024 * 1024
        ),
        name="attend",
    )(doc_lengths, queries, keys_in, values, out_grad)
    rows = pl.BlockSpec((PIECE // 2, PIECES * HEAD_DIM), lambda i: (i, 0))
    return pl.pallas_call(
        place, grid=(2,), out_shape=(out,) * 4, in_specs=[rows] * 4, out_specs=(rows,) * 4, name="place"
    )(*results)


def solution(mesh):
    tokens = P(("ctx", "head"), None)
    return jax.shard_map(
        body,
        mesh=mesh,
        in_specs=(tokens,) * 4 + (P(),),
        out_specs=(tokens,) * 4,
        check_vma=False,
    )
```
